512 devices in a mesh: cfg: 2 (over core), tp: 16 (over y, x), dp: 16 (over z).
Axes of the slice: x: 4, y: 4, z: 16, core: 2. Of those that a mesh axis runs over, the one named last changes fastest.
Arguments:
- hidden_in: bfloat16 [2, 512, 2048], P('cfg', 'dp', 'tp'), may hold values from -6 to 6
- attn_gain: float32 [2048], replicated, may hold values from 0.25 to 1.75
- w_qkv: bfloat16 [2048, 3, 2048], P(None, None, 'tp'), may hold values from -3 to 3
- w_out: bfloat16 [2048, 2048], P('tp'), may hold values from -0.125 to 0.125
- cache_keys: bfloat16 [2, 512, 128, 2048], P('cfg', 'dp', None, 'tp'), may hold values from -11 to 11
- cache_values: bfloat16 [2, 512, 128, 2048], P('cfg', 'dp', None, 'tp'), may hold values from -6 to 6
- cache_len: int32 [512], P('dp'), may hold values from 33 to 128
- text_len: int32 [512], P('dp'), may hold values from 1 to 31
- final_gain: float32 [2048], replicated, may hold values from 0.25 to 1.75
- lm_head: bfloat16 [4, 2048, 2048], P(None, 'dp', 'tp'), may hold values from -12 to 12
- guidance: float32 [512], P('dp'), may hold values from 1.5 to 4
- uniforms: float32 [512, 4, 2048], P('dp', 'cfg', 'tp'), may hold values from 1e-06 to 0.999999
Outputs:
- sample_logprobs: float32 [512, 4, 2048], P('dp', 'cfg', 'tp')
- residual_out: bfloat16 [2, 512, 2048], P('cfg', 'dp', 'tp')
The draws below stay inside these ranges and needn't reach their ends.
Inputs may be any that keep to these rules, and one draw needn't show every extreme that they name: text_len of a stream is below its cache_len.
All inputs are finite; a program needn't handle non-finite values.
Results may differ from the reference program's by a relative error of at most 0.0023.
The reference program's roundings to bfloat16 on the way (of `tokens_norm`, `projections`, `weights`, `attended` and `normed`) count: a program that leaves them out, or rounds other values in their place, can miss the bound.
Values may be sent and summed in bfloat16 or wider, within the bound.
No kernel may reach another device: no remote copies, remote signals or barrier semaphores. Data moves between devices by JAX's collectives and lax.ppermute only.
A program may use at most 64 MiB of HBM per device.

```python
import math
import jax
import jax.numpy as jnp
from jax import lax

D = 2048
HEADS = 32
HEAD_DIM = 64
CB = 4
VOCAB = 2048
CACHE = 128
STREAMS = 512


def shared_pattern(key):
    base = jax.random.fold_in(key, 7001)
    pattern = jnp.clip(jax.random.normal(jax.random.fold_in(base, 1), (D,), jnp.float32), -2.0, 2.0)
    directions = jnp.clip(jax.random.normal(jax.random.fold_in(base, 2), (HEADS, HEAD_DIM), jnp.float32), -2.0, 2.0)
    stream_order = jax.random.permutation(jax.random.fold_in(base, 3), STREAMS)
    chosen = stream_order < max(STREAMS // 8, 1)
    stream_lift = jax.random.uniform(jax.random.fold_in(base, 4), (STREAMS,), jnp.float32, 0.4, 0.95)
    strength = jnp.where(chosen, stream_lift, 0.0)
    head_order = jax.random.permutation(jax.random.fold_in(base, 5), HEADS)
    head_lift = jax.random.uniform(jax.random.fold_in(base, 6), (HEADS,), jnp.float32, 0.3, 1.3)
    head_strength = jnp.where(head_order < HEADS // 2, head_lift, 0.0)
    return (pattern, directions, strength, head_strength)


def unit_noise(key, shape):
    return jnp.clip(jax.random.normal(key, shape, jnp.float32), -6.0, 6.0)


def draw_hidden_in(key, part):
    pattern, directions, strength, head_strength = shared_pattern(key)
    noise = unit_noise(jax.random.fold_in(key, 11), (2, STREAMS, D))
    lift = strength[None, :, None]
    rows = 2.5 * lift * pattern[None, None, :] + jnp.sqrt(1.0 - lift * lift) * noise
    return jnp.clip(rows, -6.0, 6.0).astype(jnp.bfloat16)


def draw_w_qkv(key, part):
    pattern, directions, strength, head_strength = shared_pattern(key)
    noise = jnp.clip(unit_noise(jax.random.fold_in(key, 21), (D, 3, HEADS * HEAD_DIM)), -4.0, 4.0) / math.sqrt(D)
    spike = (20.0 / D * head_strength[:, None] * directions).reshape(HEADS * HEAD_DIM)
    query_part = pattern[:, None] * spike[None, :]
    slot_mask = (jnp.arange(3) == 0).astype(jnp.float32)
    whole = noise + query_part[:, None, :] * slot_mask[None, :, None]
    return jnp.clip(whole, -3.0, 3.0).astype(jnp.bfloat16)


def draw_cache_keys(key, part):
    pattern, directions, strength, head_strength = shared_pattern(key)
    noise = unit_noise(jax.random.fold_in(key, 31), (2, STREAMS, CACHE, HEADS * HEAD_DIM))
    reach = 20.0 / math.sqrt(HEAD_DIM)
    apart = 1.008
    positions = jnp.arange(CACHE)
    at_first = positions == CACHE // 4 - 1
    at_second = positions == CACHE // 4
    factor = jnp.where(at_first, reach, jnp.where(at_second, reach * apart, 0.0))
    marked = at_first | at_second
    flat_dir = directions.reshape(HEADS * HEAD_DIM)
    aligned = factor[:, None] * flat_dir[None, :]
    keys = jnp.where(marked[None, None, :, None], aligned[None, None, :, :] + 0.05 * noise, noise)
    return jnp.clip(keys, -11.0, 11.0).astype(jnp.bfloat16)


def draw_lm_head(key, part):
    pattern, directions, strength, head_strength = shared_pattern(key)
    noise = jnp.clip(unit_noise(jax.random.fold_in(key, 41), (CB, D, VOCAB)), -4.0, 4.0) / math.sqrt(D)
    chosen = jnp.stack([jax.random.permutation(jax.random.fold_in(key, 50 + codebook), VOCAB) < 8 for codebook in range(CB)])
    code_lift = jax.random.uniform(jax.random.fold_in(key, 42), (CB, VOCAB), jnp.float32, 0.94, 1.0)
    alpha = jnp.where(chosen, 360.0 / D * code_lift, 0.0)
    whole = noise + alpha[:, None, :] * pattern[None, :, None]
    return jnp.clip(whole, -12.0, 12.0).astype(jnp.bfloat16)


def plant(values, key, smallest, high):
    dims = values.shape
    index_at = [jax.random.randint(jax.random.fold_in(key, axis), (), 0, dims[axis]) for axis in range(len(dims))]
    values = values.at[tuple(index_at)].set(smallest)
    longest = dims.index(max(dims))
    index_at[longest] = (index_at[longest] + 1) % dims[longest]
    return values.at[tuple(index_at)].set(high)


def levels(key, extent, shards, least, high):
    gain, own = 1.0, jax.random.fold_in(key, 6)
    for axis_at, parts in shards:
        heights = jnp.exp(jax.random.uniform(jax.random.fold_in(own, axis_at), (parts,), jnp.float32, least / len(shards), high / len(shards)))
        gain = gain * jnp.repeat(heights, extent[axis_at] // parts).reshape([-1 if axis == axis_at else 1 for axis in range(len(extent))])
    return gain


def bell_draw(stream_key, extent, width, most, split=(), kind=jnp.bfloat16):
    entries = width * jax.random.normal(stream_key, extent, jnp.float32)
    if split:
        entries = entries * levels(stream_key, extent, split, -0.22, 0.18)
    return jnp.clip(entries, -most, most).astype(kind)


def setup_inputs(seed: int = 0) -> dict:
    key_list = jax.random.split(jax.random.key(seed), 13)
    return {
        "hidden_in": draw_hidden_in(jax.random.fold_in(key_list[12], 71), 0),
        "attn_gain": jnp.clip(1.0 + 0.15 * jax.random.normal(key_list[1], (D,), jnp.float32), 0.25, 1.75),
        "w_qkv": draw_w_qkv(jax.random.fold_in(key_list[12], 71), 0),
        "w_out": bell_draw(key_list[3], (HEADS * HEAD_DIM, D), (HEADS * HEAD_DIM) ** -0.5, 0.125, ((0, 16),)),
        "cache_keys": draw_cache_keys(jax.random.fold_in(key_list[12], 71), 0),
        "cache_values": bell_draw(key_list[5], (2, STREAMS, CACHE, HEADS * HEAD_DIM), 1.0, 6.0, ((0, 2), (1, 16), (3, 16))),
        "cache_len": plant(jax.random.randint(key_list[6], (STREAMS,), CACHE // 4 + 1, CACHE + 1), jax.random.fold_in(key_list[6], 1), CACHE // 4 + 1, CACHE).astype(jnp.int32),
        "text_len": plant(jax.random.randint(key_list[7], (STREAMS,), 1, CACHE // 4), jax.random.fold_in(key_list[7], 1), 1, (CACHE // 4) - 1).astype(jnp.int32),
        "final_gain": jnp.clip(1.0 + 0.15 * jax.random.normal(key_list[8], (D,), jnp.float32), 0.25, 1.75),
        "lm_head": draw_lm_head(jax.random.fold_in(key_list[12], 71), 0),
        "guidance": jnp.clip(1.5 + 2.5 * jax.random.uniform(key_list[10], (STREAMS,), jnp.float32) ** levels(key_list[10], (STREAMS,), ((0, 16),), -0.2, 0.2), 1.5, 4.0),
        "uniforms": jnp.clip(9.999999974752427e-07 + 0.999998 * jax.random.uniform(key_list[11], (STREAMS, CB, VOCAB), jnp.float32) ** levels(key_list[11], (STREAMS, CB, VOCAB), ((0, 16), (1, 2), (2, 16)), -0.2, 0.2), 9.999999974752427e-07, 0.999999),
    }


epsilon = 1e-05
far_below = -1e+30

def layer_norm(values_in, gain_vec):
    average = lax.optimization_barrier(jnp.mean(values_in, axis=-1, keepdims=True))
    spread = lax.optimization_barrier(jnp.mean((values_in - average) ** 2, axis=-1, keepdims=True))
    return (values_in - average) * lax.rsqrt(spread + epsilon) * gain_vec

def reference(hidden_in, attn_gain, w_qkv, w_out, cache_keys, cache_values, cache_len, text_len, final_gain, lm_head, guidance, uniforms):
    positions = jnp.arange(CACHE, dtype=jnp.int32)
    inv_root = 1.0 / HEAD_DIM ** 0.5
    residuals = []
    logit_list = []
    for branch in range(2):
        tokens_in = hidden_in[branch].astype(jnp.float32)
        tokens_norm = layer_norm(tokens_in, attn_gain).astype(jnp.bfloat16)
        projections = jnp.dot(tokens_norm, w_qkv.reshape(D, 3 * HEADS * HEAD_DIM), preferred_element_type=jnp.float32)
        projections = projections.astype(jnp.bfloat16).reshape(STREAMS, 3, HEADS, HEAD_DIM).astype(jnp.float32)
        queries = projections[:, 0]
        new_keys = projections[:, 1]
        new_values = projections[:, 2]
        key_rows = cache_keys[branch].astype(jnp.float32).reshape(STREAMS, CACHE, HEADS, HEAD_DIM)
        scores = jnp.einsum('shd,sjhd->shj', queries, key_rows) * inv_root
        usable = positions[None, :] < cache_len[:, None]
        if branch == 1:
            usable = usable & (positions[None, :] >= text_len[:, None])
        scores = jnp.where(usable[:, None, :], scores, far_below)
        self_score = lax.optimization_barrier(jnp.sum(queries * new_keys, axis=-1)) * inv_root
        peak = jnp.maximum(lax.optimization_barrier(jnp.max(scores, axis=-1)), self_score)
        raw_weights = jnp.exp(scores - peak[..., None])
        self_raw = jnp.exp(self_score - peak)
        denom = lax.optimization_barrier(jnp.sum(raw_weights, axis=-1)) + self_raw
        weights = (raw_weights / denom[..., None]).astype(jnp.bfloat16).astype(jnp.float32)
        self_weight = (self_raw / denom).astype(jnp.bfloat16).astype(jnp.float32)
        value_rows = cache_values[branch].astype(jnp.float32).reshape(STREAMS, CACHE, HEADS, HEAD_DIM)
        attended = jnp.einsum('shj,sjhd->shd', weights, value_rows) + self_weight[..., None] * new_values
        attended = attended.astype(jnp.bfloat16).reshape(STREAMS, HEADS * HEAD_DIM)
        projected = jnp.dot(attended, w_out, preferred_element_type=jnp.float32)
        residual = (tokens_in + projected).astype(jnp.bfloat16)
        residuals.append(residual)
        normed = layer_norm(residual.astype(jnp.float32), final_gain).astype(jnp.bfloat16)
        logits = jnp.einsum('sd,cdv->scv', normed.astype(jnp.float32), lm_head.astype(jnp.float32))
        logit_list.append(logits)
    conditioned = logit_list[0]
    unconditioned = logit_list[1]
    guided = unconditioned + guidance[:, None, None] * (conditioned - unconditioned)
    perturbed = guided - jnp.log(-jnp.log(uniforms))
    peak_code = lax.optimization_barrier(jnp.max(perturbed, axis=-1, keepdims=True))
    log_total = jnp.log(lax.optimization_barrier(jnp.sum(jnp.exp(perturbed - peak_code), axis=-1, keepdims=True))) + peak_code
    return (perturbed - log_total, jnp.stack(residuals))
```

```python
import jax
import jax.numpy as jnp
from jax import lax
from jax.sharding import PartitionSpec as P

D = 2048
HEAD_DIM = 64
CB = 4
CACHE = 128

epsilon = 1e-05
far_below = -1e30


def exchange(blocks, axis):
    return lax.all_to_all(blocks, axis, split_axis=0, concat_axis=0, tiled=True)


def sent_to_all(array, axis):
    return exchange(jnp.broadcast_to(array, (lax.axis_size(axis), *array.shape)), axis)


def shifted(array, axis, by):
    count = lax.axis_size(axis)
    return lax.ppermute(array, axis, [(k, (k + by) % count) for k in range(count)])


def layer_norm(values_in, gain_vec):
    average = jnp.mean(values_in, axis=-1, keepdims=True)
    spread = jnp.mean((values_in - average) ** 2, axis=-1, keepdims=True)
    return (values_in - average) * lax.rsqrt(spread + epsilon) * gain_vec


OFFSETS = (0, -4, 4, -1, -5, 3, 1, -3, 5, 8, 9, 2, 6, 7, -2, -6)


def gathered_heads(block):
    near = [block, shifted(block, "dp", 4), shifted(block, "dp", -4)]
    own = jnp.concatenate(near, 0)
    size = block.shape[0]
    low = shifted(own, "dp", 1)
    high = shifted(own, "dp", -1)
    far = shifted(near[2], "dp", -4)
    up = jnp.concatenate([far, high[:size], high[2 * size :]], 0)
    above = shifted(up, "dp", -1)
    down = jnp.concatenate([far, low[: 2 * size]], 0)
    below = shifted(down, "dp", 1)
    return jnp.concatenate([own, low, high, far, above, below], 0)


def body(
    hidden_in,
    attn_gain,
    w_qkv,
    w_out,
    cache_keys,
    cache_values,
    cache_len,
    text_len,
    final_gain,
    lm_head,
    guidance,
    uniforms,
):
    branch_index = lax.axis_index("cfg")
    local_streams = hidden_in.shape[1]
    local_heads = w_qkv.shape[2] // HEAD_DIM
    width = hidden_in.shape[2]
    inv_root = 1.0 / HEAD_DIM**0.5
    blocks = sent_to_all(hidden_in[0], "tp")
    half_books = CB // 2
    head_half = lax.dynamic_slice_in_dim(lm_head, branch_index * half_books, half_books, 0)
    heads = gathered_heads(head_half.reshape(half_books * lm_head.shape[1], lm_head.shape[2]))

    tokens_in = jnp.moveaxis(blocks, 0, 1).reshape(local_streams, D).astype(jnp.float32)
    tokens_norm = layer_norm(tokens_in, attn_gain).astype(jnp.bfloat16)
    projections = jnp.dot(
        tokens_norm,
        w_qkv.reshape(D, 3 * local_heads * HEAD_DIM),
        preferred_element_type=jnp.float32,
    )
    projections = projections.astype(jnp.bfloat16).reshape(local_streams, 3, local_heads, HEAD_DIM)
    queries = projections[:, 0]
    new_keys = projections[:, 1]
    new_values = projections[:, 2]
    key_rows = cache_keys[0].reshape(local_streams, CACHE, local_heads, HEAD_DIM)
    value_rows = cache_values[0].reshape(local_streams, CACHE, local_heads, HEAD_DIM)
    scores = (
        jnp.einsum("shd,sjhd->shj", queries, key_rows, preferred_element_type=jnp.float32)
        * inv_root
    )
    positions = jnp.arange(CACHE, dtype=jnp.int32)
    usable = (positions[None, :] < cache_len[:, None]) & (
        (branch_index == 0) | (positions[None, :] >= text_len[:, None])
    )
    scores = jnp.where(usable[:, None, :], scores, far_below)
    self_score = (
        jnp.sum(queries.astype(jnp.float32) * new_keys.astype(jnp.float32), axis=-1) * inv_root
    )
    peak = jnp.maximum(jnp.max(scores, axis=-1), self_score)
    raw_weights = jnp.exp(scores - peak[..., None])
    self_raw = jnp.exp(self_score - peak)
    denom = jnp.sum(raw_weights, axis=-1) + self_raw
    weights = (raw_weights / denom[..., None]).astype(jnp.bfloat16)
    self_weight = (self_raw / denom).astype(jnp.bfloat16).astype(jnp.float32)
    attended = jnp.einsum("shj,sjhd->shd", weights, value_rows, preferred_element_type=jnp.float32)
    attended = attended + self_weight[..., None] * new_values.astype(jnp.float32)
    attended = attended.astype(jnp.bfloat16).reshape(local_streams, local_heads * HEAD_DIM)
    projected = jnp.dot(attended, w_out, preferred_element_type=jnp.float32).astype(jnp.bfloat16)
    shares = exchange(jnp.moveaxis(projected.reshape(local_streams, -1, width), 1, 0), "tp")
    projected_part = shares.astype(jnp.float32).sum(0)
    residual_part = (hidden_in[0].astype(jnp.float32) + projected_part).astype(jnp.bfloat16)
    partner = lax.ppermute(residual_part, "cfg", [(0, 1), (1, 0)])
    both = jnp.concatenate([residual_part, partner], 0)
    rows = sent_to_all(both, "tp")
    rows = jnp.moveaxis(rows, 0, 1).reshape(2 * local_streams, D).astype(jnp.float32)
    normed = layer_norm(rows, final_gain).astype(jnp.bfloat16)
    z = lax.axis_index("dp")
    count = lax.axis_size("dp")
    parts = jnp.moveaxis(normed.reshape(2 * local_streams, count, -1), 1, 0)
    turned = lax.dynamic_slice_in_dim(jnp.concatenate([parts, parts], 0), z, count, 0)
    ordered = jnp.stack([turned[k % count] for k in OFFSETS])
    heads = heads.reshape(count, half_books, -1, heads.shape[1])
    logits = jnp.einsum("ksd,kcdv->csv", ordered, heads, preferred_element_type=jnp.float32)
    own, other = logits[:, :local_streams], logits[:, local_streams:]
    leading = branch_index == 0
    conditioned = jnp.where(leading, own, other)
    unconditioned = jnp.where(leading, other, own)
    guided = unconditioned + guidance[None, :, None] * (conditioned - unconditioned)
    perturbed = guided - jnp.moveaxis(jnp.log(-jnp.log(uniforms)), 1, 0)
    local_peak = jnp.max(perturbed, axis=-1)
    local_mass = jnp.sum(jnp.exp(perturbed - local_peak[..., None]), axis=-1)
    pairs = sent_to_all(jnp.concatenate([local_peak, local_mass], 0).reshape(1, -1), "tp")
    pairs = pairs.reshape(-1, 2, half_books, local_streams)
    peak_code = jnp.max(pairs[:, 0], 0)
    mass_total = jnp.sum(pairs[:, 1] * jnp.exp(pairs[:, 0] - peak_code), 0)
    log_total = jnp.log(mass_total) + peak_code
    sample_logprobs = jnp.moveaxis(perturbed - log_total[..., None], 0, 1)
    return (sample_logprobs, residual_part[None])


def solution(mesh):
    placed = (
        P("cfg", "dp", "tp"),
        P(),
        P(None, None, "tp"),
        P("tp", None),
        P("cfg", "dp", None, "tp"),
        P("cfg", "dp", None, "tp"),
        P("dp"),
        P("dp"),
        P(),
        P(None, "dp", "tp"),
        P("dp"),
        P("dp", "cfg", "tp"),
    )
    return jax.shard_map(
        body,
        mesh=mesh,
        in_specs=placed,
        out_specs=(P("dp", "cfg", "tp"), P("cfg", "dp", "tp")),
        check_vma=False,
    )
```

```python
import jax
import jax.numpy as jnp
from jax import lax
from jax.experimental import pallas as pl
from jax.experimental.pallas import tpu as pltpu
from jax.sharding import PartitionSpec as P

D = 2048
HEAD_DIM = 64
CB = 4
CACHE = 128

epsilon = 1e-05
far_below = -1e30

f32, bf16 = jnp.float32, jnp.bfloat16


def exchange(blocks, axis):
    return lax.all_to_all(blocks, axis, split_axis=0, concat_axis=0, tiled=True)


def sent_to_all(array, axis):
    return exchange(jnp.broadcast_to(array, (lax.axis_size(axis), *array.shape)), axis)


def shifted(array, axis, by):
    count = lax.axis_size(axis)
    return lax.ppermute(array, axis, [(k, (k + by) % count) for k in range(count)])


PIECES = (
    (0,),
    (-6,),
    (6,),
    (-3, -9),
    (3, 9),
    (-1, -4, 2, 5, 8),
    (1, 4, -2, -5),
)


def first_heads(block):
    return block, shifted(block, "dp", 6), shifted(block, "dp", -6)


def second_heads(block, from_low, from_high):
    low = shifted(jnp.concatenate([block, from_low], 0), "dp", 3)
    high = shifted(jnp.concatenate([block, from_high], 0), "dp", -3)
    return low, high


def third_heads(block, from_low, from_high, low, high):
    size = block.shape[0]
    below = [block, low[:size], high[:size], from_high, high[size:]]
    above = [block, high[:size], low[:size], from_low]
    below = shifted(jnp.concatenate(below, 0), "dp", 1)
    above = shifted(jnp.concatenate(above, 0), "dp", -1)
    return below, above


def normalized(rows, gain):
    count = rows.shape[0] * rows.shape[2]
    average = jnp.sum(jnp.sum(rows, 0), -1, keepdims=True) / count
    apart = rows - average[None]
    spread = jnp.sum(jnp.sum(apart * apart, 0), -1, keepdims=True) / count
    return (apart * lax.rsqrt(spread + epsilon)[None] * gain).astype(bf16)


def side_by_side(blocks):
    return jnp.concatenate(blocks, axis=-1)


def attend_kernel(
    blocks_ref,
    small_ref,
    qkv_in,
    keys_in,
    values_in,
    out_w_in,
    parts_ref,
    qkv_ref,
    keys_ref,
    values_ref,
    out_w_ref,
    arrived,
):
    count, streams, width = blocks_ref.shape
    copies = [
        pltpu.make_async_copy(source, target, arrived.at[k])
        for k, (source, target) in enumerate(
            (
                (qkv_in, qkv_ref),
                (keys_in, keys_ref),
                (values_in, values_ref),
                (out_w_in, out_w_ref),
            )
        )
    ]
    for copy in copies:
        copy.start()
    gain = small_ref[streams:][:, None, :]
    tokens = normalized(blocks_ref[...].astype(f32), gain)
    tokens = side_by_side([tokens[k] for k in range(count)])
    copies[0].wait()
    query, new_key, new_value = (
        jnp.dot(tokens, qkv_ref[slot], preferred_element_type=f32).astype(bf16).astype(f32)
        for slot in range(3)
    )
    head_of_lane = lax.broadcasted_iota(jnp.int32, (8, width), 1) // HEAD_DIM
    own_head = (head_of_lane == lax.broadcasted_iota(jnp.int32, (8, width), 0)).astype(f32)
    queries = query[:, None, :] * own_head[None]
    inv_root = 1.0 / HEAD_DIM**0.5
    copies[1].wait()
    scores = (
        lax.dot_general(
            queries.astype(bf16),
            keys_ref[...],
            (((2,), (2,)), ((0,), (0,))),
            preferred_element_type=f32,
        )
        * inv_root
    )
    scores = jnp.where(small_ref[:streams][:, None, :] > 0, scores, far_below)
    self_score = jnp.sum(queries * new_key[:, None, :], -1, keepdims=True) * inv_root
    peak = jnp.maximum(jnp.max(scores, -1, keepdims=True), self_score)
    raw = jnp.exp(scores - peak)
    self_raw = jnp.exp(self_score - peak)
    denom = jnp.sum(raw, -1, keepdims=True) + self_raw
    weights = (raw / denom).astype(bf16)
    self_weight = (self_raw / denom).astype(bf16).astype(f32)
    copies[2].wait()
    attended = lax.dot_general(
        weights, values_ref[...], (((2,), (1,)), ((0,), (0,))), preferred_element_type=f32
    )
    attended = (attended + self_weight * new_value[:, None, :]) * own_head[None]
    attended = jnp.sum(attended, 1).astype(bf16)
    copies[3].wait()
    projected = jnp.dot(attended, out_w_ref[...], preferred_element_type=f32)
    for k in range(count):
        parts_ref[k] = projected[:, k * width : (k + 1) * width]


def norm_kernel(rows_ref, gain_ref, normed_ref):
    normed_ref[...] = normalized(rows_ref[...].astype(f32), gain_ref[...])


def logits_kernel(place_ref, normed_ref, guidance_ref, noise_ref, *refs):
    piece_refs, (perturbed_ref, mass_ref) = refs[: len(PIECES)], refs[len(PIECES) :]
    count = normed_ref.shape[0]
    streams = noise_ref.shape[0]
    z, branch = place_ref[0], place_ref[1]
    total = None
    for offsets, piece_ref in zip(PIECES, piece_refs):
        rows = side_by_side([normed_ref[lax.rem(z + k + count, count)] for k in offsets])
        part = jnp.dot(rows, piece_ref[...], preferred_element_type=f32)
        total = part if total is None else total + part
    own, other = total[:streams], total[streams:]
    conditioned = jnp.where(branch == 0, own, other)
    unconditioned = jnp.where(branch == 0, other, own)
    guided = unconditioned + guidance_ref[...] * (conditioned - unconditioned)
    perturbed = guided + noise_ref[...]
    perturbed_ref[...] = perturbed
    width = perturbed.shape[1] // 2
    lane = lax.broadcasted_iota(jnp.int32, (width, width), 1)
    columns = jnp.zeros((width, width), f32)
    for book in range(2):
        codes = perturbed[:, book * width : (book + 1) * width]
        peak = jnp.max(codes, -1, keepdims=True)
        mass = jnp.log(jnp.sum(jnp.exp(codes - peak), -1, keepdims=True)) + peak
        mass = jnp.concatenate([mass, jnp.zeros((width - streams, 1), f32)], 0)
        columns = jnp.where(lane == book, mass, columns)
    mass = columns.T[:8]
    for k in range(count):
        mass_ref[k] = mass


def final_kernel(mass_ref, perturbed_ref, out_ref):
    streams = perturbed_ref.shape[0]
    masses = mass_ref[...]
    peak = jnp.max(masses, 0)
    total = jnp.log(jnp.sum(jnp.exp(masses - peak[None]), 0)) + peak
    width = total.shape[1]
    total = jnp.concatenate([total, jnp.zeros((width - 8, width), f32)], 0).T
    for book in range(2):
        codes = perturbed_ref[:, book * width : (book + 1) * width]
        out_ref[:, book, :] = codes - total[:streams, book : book + 1]


def vmem(count):
    return [pl.BlockSpec(memory_space=pltpu.VMEM)] * count


def body(
    hidden_in,
    attn_gain,
    w_qkv,
    w_out,
    cache_keys,
    cache_values,
    cache_len,
    text_len,
    final_gain,
    lm_head,
    guidance,
    uniforms,
):
    branch_index = lax.axis_index("cfg")
    z = lax.axis_index("dp")
    count = lax.axis_size("tp")
    streams, width = hidden_in.shape[1:]
    half_books = CB // 2
    blocks = sent_to_all(hidden_in[0], "tp")
    head_half = lax.dynamic_slice_in_dim(lm_head, branch_index * half_books, half_books, 0)
    heads = first_heads(jnp.moveaxis(head_half, 0, 1).reshape(lm_head.shape[1], -1))
    positions = jnp.arange(CACHE, dtype=jnp.int32)
    usable = (positions[None, :] < cache_len[:, None]) & (
        (branch_index == 0) | (positions[None, :] >= text_len[:, None])
    )
    small = jnp.concatenate([usable.astype(f32), attn_gain.reshape(count, width)], 0)
    noise = -jnp.log(-jnp.log(uniforms)).reshape(streams, half_books * width)
    parts = pl.pallas_call(
        attend_kernel,
        out_shape=jax.ShapeDtypeStruct((count, streams, width), f32),
        in_specs=vmem(2) + [pl.BlockSpec(memory_space=pltpu.HBM)] * 4,
        out_specs=pl.BlockSpec(memory_space=pltpu.VMEM),
        scratch_shapes=[
            pltpu.VMEM((3, D, width), bf16),
            pltpu.VMEM(cache_keys.shape[1:], bf16),
            pltpu.VMEM(cache_values.shape[1:], bf16),
            pltpu.VMEM(w_out.shape, bf16),
            pltpu.SemaphoreType.DMA((4,)),
        ],
        compiler_params=pltpu.CompilerParams(vmem_limit_bytes=54600 << 10),
        cost_estimate=pl.CostEstimate(flops=2 * 10**10, bytes_accessed=50 << 20, transcendentals=10**5),
    )(
        blocks,
        small,
        jnp.moveaxis(w_qkv, 1, 0),
        cache_keys[0],
        cache_values[0],
        w_out,
    )
    parts, heads = lax.optimization_barrier((parts, heads))
    shares = exchange(parts, "tp")
    heads += second_heads(*heads)
    residual_part = (hidden_in[0].astype(f32) + shares.sum(0)).astype(bf16)
    partner = lax.ppermute(residual_part, "cfg", [(0, 1), (1, 0)])
    both = jnp.concatenate([residual_part, partner], 0)
    both, heads = lax.optimization_barrier((both, heads))
    rows = sent_to_all(both, "tp")
    heads += third_heads(*heads)
    normed = pl.pallas_call(
        norm_kernel,
        out_shape=jax.ShapeDtypeStruct(rows.shape, bf16),
        in_specs=vmem(2),
        out_specs=vmem(1)[0],
        compiler_params=pltpu.CompilerParams(vmem_limit_bytes=8 << 20),
        cost_estimate=pl.CostEstimate(flops=2 * 10**10, bytes_accessed=50 << 20, transcendentals=64),
    )(rows, final_gain.reshape(count, 1, width))
    perturbed, mass = pl.pallas_call(
        logits_kernel,
        out_shape=(
            jax.ShapeDtypeStruct((streams, half_books * width), f32),
            jax.ShapeDtypeStruct((count, 8, width), f32),
        ),
        in_specs=[pl.BlockSpec(memory_space=pltpu.SMEM)] + vmem(3 + len(heads)),
        out_specs=tuple(vmem(2)),
        compiler_params=pltpu.CompilerParams(vmem_limit_bytes=8 << 20),
        cost_estimate=pl.CostEstimate(flops=10**8, bytes_accessed=2 << 20, transcendentals=10**4),
    )(
        jnp.stack([z, branch_index]).astype(jnp.int32),
        normed,
        guidance[:, None],
        noise,
        *heads,
    )
    masses = exchange(mass, "tp")
    sample_logprobs = pl.pallas_call(
        final_kernel,
        out_shape=jax.ShapeDtypeStruct((streams, half_books, width), f32),
        in_specs=vmem(2),
        out_specs=pl.BlockSpec(memory_space=pltpu.VMEM),
        compiler_params=pltpu.CompilerParams(vmem_limit_bytes=8 << 20),
    )(masses, perturbed)
    return (sample_logprobs, residual_part[None])


def solution(mesh):
    placed = (
        P("cfg", "dp", "tp"),
        P(),
        P(None, None, "tp"),
        P("tp", None),
        P("cfg", "dp", None, "tp"),
        P("cfg", "dp", None, "tp"),
        P("dp"),
        P("dp"),
        P(),
        P(None, "dp", "tp"),
        P("dp"),
        P("dp", "cfg", "tp"),
    )
    return jax.shard_map(
        body,
        mesh=mesh,
        in_specs=placed,
        out_specs=(P("dp", "cfg", "tp"), P("cfg", "dp", "tp")),
        check_vma=False,
    )
```

```python
import jax
import jax.numpy as jnp
from jax import lax
from jax.experimental import pallas as pl
from jax.experimental.pallas import tpu as pltpu
from jax.sharding import PartitionSpec as P

D = 2048
HEAD_DIM = 64
CB = 4
CACHE = 128

epsilon = 1e-05
far_below = -1e30

f32, bf16 = jnp.float32, jnp.bfloat16


def exchange(blocks, axis):
    return lax.all_to_all(blocks, axis, split_axis=0, concat_axis=0, tiled=True)


def sent_to_all(array, axis):
    return exchange(jnp.broadcast_to(array, (lax.axis_size(axis), *array.shape)), axis)


def shifted(array, axis, by):
    count = lax.axis_size(axis)
    return lax.ppermute(array, axis, [(k, (k + by) % count) for k in range(count)])


PIECES = (
    (0,),
    (-8,),
    (3, -5),
    (-2, 6),
    (2, -6, -3, 5, -1),
    (1, -7, 4, -4, 7),
)


def first_heads(block):
    return block, shifted(block, "dp", 8)


def second_heads(block, opposite):
    both = jnp.concatenate([block, opposite], 0)
    return shifted(both, "dp", -3), shifted(both, "dp", 2)


def third_heads(block, opposite, high, low):
    size = block.shape[0]
    below = jnp.concatenate([high, low, block], 0)
    above = jnp.concatenate([block, opposite, high, low[size:]], 0)
    return shifted(below, "dp", 1), shifted(above, "dp", -1)


def normalized(rows, gain):
    count = rows.shape[0] * rows.shape[2]
    average = jnp.sum(jnp.sum(rows, 0), -1, keepdims=True) / count
    apart = rows - average[None]
    spread = jnp.sum(jnp.sum(apart * apart, 0), -1, keepdims=True) / count
    return (apart * lax.rsqrt(spread + epsilon)[None] * gain).astype(bf16)


def side_by_side(blocks):
    return jnp.concatenate(blocks, axis=-1)


def attend_kernel(
    blocks_ref,
    small_ref,
    qkv_in,
    keys_in,
    values_in,
    out_w_in,
    parts_ref,
    qkv_ref,
    keys_ref,
    values_ref,
    out_w_ref,
    arrived,
):
    count, streams, width = blocks_ref.shape
    copies = [
        pltpu.make_async_copy(source, target, arrived.at[k])
        for k, (source, target) in enumerate(
            (
                (qkv_in, qkv_ref),
                (keys_in, keys_ref),
                (values_in, values_ref),
                (out_w_in, out_w_ref),
            )
        )
    ]
    for copy in copies:
        copy.start()
    gain = small_ref[streams:][:, None, :]
    tokens = normalized(blocks_ref[...].astype(f32), gain)
    tokens = side_by_side([tokens[k] for k in range(count)])
    copies[0].wait()
    query, new_key, new_value = (
        jnp.dot(tokens, qkv_ref[slot], preferred_element_type=f32).astype(bf16).astype(f32)
        for slot in range(3)
    )
    head_of_lane = lax.broadcasted_iota(jnp.int32, (8, width), 1) // HEAD_DIM
    own_head = (head_of_lane == lax.broadcasted_iota(jnp.int32, (8, width), 0)).astype(f32)
    queries = query[:, None, :] * own_head[None]
    inv_root = 1.0 / HEAD_DIM**0.5
    copies[1].wait()
    scores = (
        lax.dot_general(
            queries.astype(bf16),
            keys_ref[...],
            (((2,), (2,)), ((0,), (0,))),
            preferred_element_type=f32,
        )
        * inv_root
    )
    scores = jnp.where(small_ref[:streams][:, None, :] > 0, scores, far_below)
    self_score = jnp.sum(queries * new_key[:, None, :], -1, keepdims=True) * inv_root
    peak = jnp.maximum(jnp.max(scores, -1, keepdims=True), self_score)
    raw = jnp.exp(scores - peak)
    self_raw = jnp.exp(self_score - peak)
    denom = jnp.sum(raw, -1, keepdims=True) + self_raw
    weights = (raw / denom).astype(bf16)
    self_weight = (self_raw / denom).astype(bf16).astype(f32)
    copies[2].wait()
    attended = lax.dot_general(
        weights, values_ref[...], (((2,), (1,)), ((0,), (0,))), preferred_element_type=f32
    )
    attended = (attended + self_weight * new_value[:, None, :]) * own_head[None]
    attended = jnp.sum(attended, 1).astype(bf16)
    copies[3].wait()
    projected = jnp.dot(attended, out_w_ref[...], preferred_element_type=f32)
    for k in range(count):
        parts_ref[k] = projected[:, k * width : (k + 1) * width]


def norm_kernel(rows_ref, gain_ref, normed_ref):
    count = gain_ref.shape[0]
    for branch in range(2):
        rows = rows_ref[branch * count : (branch + 1) * count].astype(f32)
        normed_ref[branch] = normalized(rows, gain_ref[...])


def logits_kernel(place_ref, normed_ref, guidance_ref, noise_ref, *refs):
    piece_refs, (perturbed_ref, mass_ref) = refs[: len(PIECES)], refs[len(PIECES) :]
    count = normed_ref.shape[1]
    streams = noise_ref.shape[0]
    z = place_ref[0]
    total = None
    for offsets, piece_ref in zip(PIECES, piece_refs):
        at = [lax.rem(z + k + count, count) for k in offsets]
        rows = [side_by_side([normed_ref[branch, k] for k in at]) for branch in range(2)]
        rows = jnp.concatenate(rows, 0)
        part = jnp.dot(rows, piece_ref[...], preferred_element_type=f32)
        total = part if total is None else total + part
    conditioned, unconditioned = total[:streams], total[streams:]
    guided = unconditioned + guidance_ref[...] * (conditioned - unconditioned)
    perturbed = guided + noise_ref[...]
    perturbed_ref[...] = perturbed
    width = perturbed.shape[1] // 2
    lane = lax.broadcasted_iota(jnp.int32, (width, width), 1)
    columns = jnp.zeros((width, width), f32)
    for book in range(2):
        codes = perturbed[:, book * width : (book + 1) * width]
        peak = jnp.max(codes, -1, keepdims=True)
        mass = jnp.log(jnp.sum(jnp.exp(codes - peak), -1, keepdims=True)) + peak
        mass = jnp.concatenate([mass, jnp.zeros((width - streams, 1), f32)], 0)
        columns = jnp.where(lane == book, mass, columns)
    mass = columns.T[:8]
    for k in range(count):
        mass_ref[k] = mass


def final_kernel(mass_ref, perturbed_ref, out_ref):
    streams = perturbed_ref.shape[0]
    masses = mass_ref[...]
    peak = jnp.max(masses, 0)
    total = jnp.log(jnp.sum(jnp.exp(masses - peak[None]), 0)) + peak
    width = total.shape[1]
    total = jnp.concatenate([total, jnp.zeros((width - 8, width), f32)], 0).T
    for book in range(2):
        codes = perturbed_ref[:, book * width : (book + 1) * width]
        out_ref[:, book, :] = codes - total[:streams, book : book + 1]


def vmem(count):
    return [pl.BlockSpec(memory_space=pltpu.VMEM)] * count


def body(
    hidden_in,
    attn_gain,
    w_qkv,
    w_out,
    cache_keys,
    cache_values,
    cache_len,
    text_len,
    final_gain,
    lm_head,
    guidance,
    uniforms,
):
    branch_index = lax.axis_index("cfg")
    z = lax.axis_index("dp")
    count = lax.axis_size("tp")
    streams, width = hidden_in.shape[1:]
    half_books = CB // 2
    blocks = sent_to_all(hidden_in[0], "tp")
    positions = jnp.arange(CACHE, dtype=jnp.int32)
    usable = (positions[None, :] < cache_len[:, None]) & (
        (branch_index == 0) | (positions[None, :] >= text_len[:, None])
    )
    small = jnp.concatenate([usable.astype(f32), attn_gain.reshape(count, width)], 0)
    head_half = lax.dynamic_slice_in_dim(lm_head, branch_index * half_books, half_books, 0)
    small, head_half = lax.optimization_barrier((small, head_half))
    heads = first_heads(jnp.moveaxis(head_half, 0, 1).reshape(lm_head.shape[1], -1))
    noise = -jnp.log(-jnp.log(uniforms)).reshape(streams, half_books * width)
    parts = pl.pallas_call(
        attend_kernel,
        out_shape=jax.ShapeDtypeStruct((count, streams, width), f32),
        in_specs=vmem(2) + [pl.BlockSpec(memory_space=pltpu.HBM)] * 4,
        out_specs=pl.BlockSpec(memory_space=pltpu.VMEM),
        scratch_shapes=[
            pltpu.VMEM((3, D, width), bf16),
            pltpu.VMEM(cache_keys.shape[1:], bf16),
            pltpu.VMEM(cache_values.shape[1:], bf16),
            pltpu.VMEM(w_out.shape, bf16),
            pltpu.SemaphoreType.DMA((4,)),
        ],
        compiler_params=pltpu.CompilerParams(vmem_limit_bytes=54600 << 10),
        cost_estimate=pl.CostEstimate(flops=2 * 10**11, bytes_accessed=50 << 20, transcendentals=10**5),
    )(
        blocks,
        small,
        jnp.moveaxis(w_qkv, 1, 0),
        cache_keys[0],
        cache_values[0],
        w_out,
    )
    parts, heads = lax.optimization_barrier((parts, heads))
    shares = exchange(parts, "tp")
    heads += second_heads(*heads)
    residual_part = (hidden_in[0].astype(f32) + shares.sum(0)).astype(bf16)
    rows = sent_to_all(residual_part, ("cfg", "tp"))
    heads += third_heads(*heads)
    normed = pl.pallas_call(
        norm_kernel,
        out_shape=jax.ShapeDtypeStruct((2, count, streams, width), bf16),
        in_specs=vmem(2),
        out_specs=vmem(1)[0],
        compiler_params=pltpu.CompilerParams(vmem_limit_bytes=8 << 20),
        cost_estimate=pl.CostEstimate(flops=2 * 10**10, bytes_accessed=50 << 20, transcendentals=64),
    )(rows, final_gain.reshape(count, 1, width))
    perturbed, mass = pl.pallas_call(
        logits_kernel,
        out_shape=(
            jax.ShapeDtypeStruct((streams, half_books * width), f32),
            jax.ShapeDtypeStruct((count, 8, width), f32),
        ),
        in_specs=[pl.BlockSpec(memory_space=pltpu.SMEM)] + vmem(3 + len(heads)),
        out_specs=tuple(vmem(2)),
        compiler_params=pltpu.CompilerParams(vmem_limit_bytes=8 << 20),
        cost_estimate=pl.CostEstimate(flops=10**8, bytes_accessed=2 << 20, transcendentals=10**4),
    )(
        z[None].astype(jnp.int32),
        normed,
        guidance[:, None],
        noise,
        *heads,
    )
    masses = exchange(mass, "tp")
    sample_logprobs = pl.pallas_call(
        final_kernel,
        out_shape=jax.ShapeDtypeStruct((streams, half_books, width), f32),
        in_specs=vmem(2),
        out_specs=pl.BlockSpec(memory_space=pltpu.VMEM),
        compiler_params=pltpu.CompilerParams(vmem_limit_bytes=8 << 20),
    )(masses, perturbed)
    return (sample_logprobs, residual_part[None])


def solution(mesh):
    placed = (
        P("cfg", "dp", "tp"),
        P(),
        P(None, None, "tp"),
        P("tp", None),
        P("cfg", "dp", None, "tp"),
        P("cfg", "dp", None, "tp"),
        P("dp"),
        P("dp"),
        P(),
        P(None, "dp", "tp"),
        P("dp"),
        P("dp", "cfg", "tp"),
    )
    return jax.shard_map(
        body,
        mesh=mesh,
        in_specs=placed,
        out_specs=(P("dp", "cfg", "tp"), P("cfg", "dp", "tp")),
        check_vma=False,
    )
```

```python
import jax
import jax.numpy as jnp
from jax import lax
from jax.experimental import pallas as pl
from jax.experimental.pallas import tpu as pltpu
from jax.sharding import PartitionSpec as P

D = 2048
HEAD_DIM = 64
CB = 4
CACHE = 128

epsilon = 1e-05
far_below = -1e30

f32, bf16 = jnp.float32, jnp.bfloat16


def exchange(blocks, axis):
    return lax.all_to_all(blocks, axis, split_axis=0, concat_axis=0, tiled=True)


def sent_to_all(array, axis):
    return exchange(jnp.broadcast_to(array, (lax.axis_size(axis), *array.shape)), axis)


PIECES = ((0,), (1,), (4, 5), (2, 3, 6, 7), (-1, -2, -5, -6), (-3, -4, -7, -8))


def moved(array, steps):
    count = lax.axis_size("dp")
    route = []
    for target in range(count):
        source = target + steps if target % 2 else target - steps
        route.append((source % count, target))
    return lax.ppermute(array, "dp", route)


def join_kernel(*refs):
    pieces, out_ref, arrived = refs[:-2], refs[-2], refs[-1]
    copies, at = [], 0
    for k, piece in enumerate(pieces):
        target = out_ref.at[pl.ds(at, piece.shape[0])]
        copies.append(pltpu.make_async_copy(piece, target, arrived.at[k]))
        at += piece.shape[0]
    for copy in copies:
        copy.start()
    for copy in copies:
        copy.wait()


def joined(*pieces):
    rows = sum(piece.shape[0] for piece in pieces)
    return pl.pallas_call(
        join_kernel,
        out_shape=jax.ShapeDtypeStruct((rows, *pieces[0].shape[1:]), pieces[0].dtype),
        in_specs=[pl.BlockSpec(memory_space=pl.ANY)] * len(pieces),
        out_specs=pl.BlockSpec(memory_space=pl.ANY),
        scratch_shapes=[pltpu.SemaphoreType.DMA((len(pieces),))],
        compiler_params=pltpu.CompilerParams(vmem_limit_bytes=8 << 20),
    )(*pieces)


def first_heads(block):
    next_one = moved(block, 1)
    return block, next_one, moved(joined(block, next_one), 4)


def second_heads(*heads):
    held = joined(*heads)
    from_same = moved(held, 2)
    return from_same, moved(held, -1)


def third_heads(from_same):
    return moved(from_same, -1)


def normalized(rows, gain):
    count = rows.shape[0] * rows.shape[2]
    average = jnp.sum(jnp.sum(rows, 0), -1, keepdims=True) / count
    apart = rows - average[None]
    spread = jnp.sum(jnp.sum(apart * apart, 0), -1, keepdims=True) / count
    return (apart * lax.rsqrt(spread + epsilon)[None] * gain).astype(bf16)


def side_by_side(blocks):
    return jnp.concatenate(blocks, axis=-1)


def attend_kernel(
    blocks_ref,
    small_ref,
    qkv_in,
    keys_in,
    values_in,
    out_w_in,
    parts_ref,
    qkv_ref,
    keys_ref,
    values_ref,
    out_w_ref,
    arrived,
):
    count, streams, width = blocks_ref.shape
    copies = [
        pltpu.make_async_copy(source, target, arrived.at[k])
        for k, (source, target) in enumerate(
            (
                (qkv_in, qkv_ref),
                (keys_in, keys_ref),
                (values_in, values_ref),
                (out_w_in, out_w_ref),
            )
        )
    ]
    for copy in copies:
        copy.start()
    gain = small_ref[streams:][:, None, :]
    tokens = normalized(blocks_ref[...].astype(f32), gain)
    tokens = side_by_side([tokens[k] for k in range(count)])
    copies[0].wait()
    query, new_key, new_value = (
        jnp.dot(tokens, qkv_ref[slot], preferred_element_type=f32).astype(bf16).astype(f32)
        for slot in range(3)
    )
    head_of_lane = lax.broadcasted_iota(jnp.int32, (8, width), 1) // HEAD_DIM
    own_head = (head_of_lane == lax.broadcasted_iota(jnp.int32, (8, width), 0)).astype(f32)
    queries = query[:, None, :] * own_head[None]
    inv_root = 1.0 / HEAD_DIM**0.5
    copies[1].wait()
    scores = (
        lax.dot_general(
            queries.astype(bf16),
            keys_ref[...],
            (((2,), (2,)), ((0,), (0,))),
            preferred_element_type=f32,
        )
        * inv_root
    )
    scores = jnp.where(small_ref[:streams][:, None, :] > 0, scores, far_below)
    self_score = jnp.sum(queries * new_key[:, None, :], -1, keepdims=True) * inv_root
    peak = jnp.maximum(jnp.max(scores, -1, keepdims=True), self_score)
    raw = jnp.exp(scores - peak)
    self_raw = jnp.exp(self_score - peak)
    denom = jnp.sum(raw, -1, keepdims=True) + self_raw
    weights = (raw / denom).astype(bf16)
    self_weight = (self_raw / denom).astype(bf16).astype(f32)
    copies[2].wait()
    attended = lax.dot_general(
        weights, values_ref[...], (((2,), (1,)), ((0,), (0,))), preferred_element_type=f32
    )
    attended = (attended + self_weight * new_value[:, None, :]) * own_head[None]
    attended = jnp.sum(attended, 1).astype(bf16)
    copies[3].wait()
    projected = jnp.dot(attended, out_w_ref[...], preferred_element_type=f32)
    for k in range(count):
        parts_ref[k] = projected[:, k * width : (k + 1) * width]


def norm_kernel(rows_ref, gain_ref, normed_ref):
    count = gain_ref.shape[0]
    for branch in range(2):
        rows = rows_ref[branch * count : (branch + 1) * count].astype(f32)
        normed_ref[branch] = normalized(rows, gain_ref[...])


def logits_kernel(place_ref, normed_ref, guidance_ref, noise_ref, *refs):
    piece_refs, (perturbed_ref, mass_ref) = refs[: len(PIECES)], refs[len(PIECES) :]
    count = normed_ref.shape[1]
    streams = noise_ref.shape[0]
    z = place_ref[0]
    upwards = 2 * lax.rem(z, 2) - 1
    total = None
    for offsets, piece_ref in zip(PIECES, piece_refs):
        at = [lax.rem(z + k * upwards + count, count) for k in offsets]
        rows = [side_by_side([normed_ref[branch, k] for k in at]) for branch in range(2)]
        rows = jnp.concatenate(rows, 0)
        part = jnp.dot(rows, piece_ref[...], preferred_element_type=f32)
        total = part if total is None else total + part
    conditioned, unconditioned = total[:streams], total[streams:]
    guided = unconditioned + guidance_ref[...] * (conditioned - unconditioned)
    perturbed = guided + noise_ref[...]
    perturbed_ref[...] = perturbed
    width = perturbed.shape[1] // 2
    lane = lax.broadcasted_iota(jnp.int32, (width, width), 1)
    columns = jnp.zeros((width, width), f32)
    for book in range(2):
        codes = perturbed[:, book * width : (book + 1) * width]
        peak = jnp.max(codes, -1, keepdims=True)
        mass = jnp.log(jnp.sum(jnp.exp(codes - peak), -1, keepdims=True)) + peak
        mass = jnp.concatenate([mass, jnp.zeros((width - streams, 1), f32)], 0)
        columns = jnp.where(lane == book, mass, columns)
    mass = columns.T[:8]
    for k in range(count):
        mass_ref[k] = mass


def final_kernel(mass_ref, perturbed_ref, out_ref):
    streams = perturbed_ref.shape[0]
    masses = mass_ref[...]
    peak = jnp.max(masses, 0)
    total = jnp.log(jnp.sum(jnp.exp(masses - peak[None]), 0)) + peak
    width = total.shape[1]
    total = jnp.concatenate([total, jnp.zeros((width - 8, width), f32)], 0).T
    for book in range(2):
        codes = perturbed_ref[:, book * width : (book + 1) * width]
        out_ref[:, book, :] = codes - total[:streams, book : book + 1]


def vmem(count):
    return [pl.BlockSpec(memory_space=pltpu.VMEM)] * count


def body(
    hidden_in,
    attn_gain,
    w_qkv,
    w_out,
    cache_keys,
    cache_values,
    cache_len,
    text_len,
    final_gain,
    lm_head,
    guidance,
    uniforms,
):
    branch_index = lax.axis_index("cfg")
    z = lax.axis_index("dp")
    count = lax.axis_size("tp")
    streams, width = hidden_in.shape[1:]
    half_books = CB // 2
    blocks = sent_to_all(hidden_in[0], "tp")
    positions = jnp.arange(CACHE, dtype=jnp.int32)
    usable = (positions[None, :] < cache_len[:, None]) & (
        (branch_index == 0) | (positions[None, :] >= text_len[:, None])
    )
    small = jnp.concatenate([usable.astype(f32), attn_gain.reshape(count, width)], 0)
    head_half = lax.dynamic_slice_in_dim(lm_head, branch_index * half_books, half_books, 0)
    heads = first_heads(jnp.moveaxis(head_half, 0, 1).reshape(lm_head.shape[1], -1))
    noise = -jnp.log(-jnp.log(uniforms)).reshape(streams, half_books * width)
    parts = pl.pallas_call(
        attend_kernel,
        out_shape=jax.ShapeDtypeStruct((count, streams, width), f32),
        in_specs=vmem(2) + [pl.BlockSpec(memory_space=pltpu.HBM)] * 4,
        out_specs=pl.BlockSpec(memory_space=pltpu.VMEM),
        scratch_shapes=[
            pltpu.VMEM((3, D, width), bf16),
            pltpu.VMEM(cache_keys.shape[1:], bf16),
            pltpu.VMEM(cache_values.shape[1:], bf16),
            pltpu.VMEM(w_out.shape, bf16),
            pltpu.SemaphoreType.DMA((4,)),
        ],
        compiler_params=pltpu.CompilerParams(vmem_limit_bytes=54600 << 10),
        cost_estimate=pl.CostEstimate(flops=2 * 10**11, bytes_accessed=50 << 20, transcendentals=10**5),
    )(
        blocks,
        small,
        jnp.moveaxis(w_qkv, 1, 0),
        cache_keys[0],
        cache_values[0],
        w_out,
    )
    parts, heads = lax.optimization_barrier((parts, heads))
    shares = exchange(parts, "tp")
    heads += second_heads(*heads)
    residual_part = (hidden_in[0].astype(f32) + shares.sum(0)).astype(bf16)
    rows = sent_to_all(residual_part, ("cfg", "tp"))
    heads += (third_heads(heads[3]),)
    normed = pl.pallas_call(
        norm_kernel,
        out_shape=jax.ShapeDtypeStruct((2, count, streams, width), bf16),
        in_specs=vmem(2),
        out_specs=vmem(1)[0],
        compiler_params=pltpu.CompilerParams(vmem_limit_bytes=8 << 20),
        cost_estimate=pl.CostEstimate(flops=2 * 10**10, bytes_accessed=50 << 20, transcendentals=64),
    )(rows, final_gain.reshape(count, 1, width))
    perturbed, mass = pl.pallas_call(
        logits_kernel,
        out_shape=(
            jax.ShapeDtypeStruct((streams, half_books * width), f32),
            jax.ShapeDtypeStruct((count, 8, width), f32),
        ),
        in_specs=[pl.BlockSpec(memory_space=pltpu.SMEM)] + vmem(3 + len(heads)),
        out_specs=tuple(vmem(2)),
        compiler_params=pltpu.CompilerParams(vmem_limit_bytes=8 << 20),
        cost_estimate=pl.CostEstimate(flops=10**8, bytes_accessed=2 << 20, transcendentals=10**4),
    )(
        z[None].astype(jnp.int32),
        normed,
        guidance[:, None],
        noise,
        *heads,
    )
    masses = exchange(mass, "tp")
    sample_logprobs = pl.pallas_call(
        final_kernel,
        out_shape=jax.ShapeDtypeStruct((streams, half_books, width), f32),
        in_specs=vmem(2),
        out_specs=pl.BlockSpec(memory_space=pltpu.VMEM),
        compiler_params=pltpu.CompilerParams(vmem_limit_bytes=8 << 20),
    )(masses, perturbed)
    return (sample_logprobs, residual_part[None])


def solution(mesh):
    placed = (
        P("cfg", "dp", "tp"),
        P(),
        P(None, None, "tp"),
        P("tp", None),
        P("cfg", "dp", None, "tp"),
        P("cfg", "dp", None, "tp"),
        P("dp"),
        P("dp"),
        P(),
        P(None, "dp", "tp"),
        P("dp"),
        P("dp", "cfg", "tp"),
    )
    return jax.shard_map(
        body,
        mesh=mesh,
        in_specs=placed,
        out_specs=(P("dp", "cfg", "tp"), P("cfg", "dp", "tp")),
        check_vma=False,
    )
```

```python
import jax
import jax.numpy as jnp
from jax import lax
from jax.experimental import pallas as pl
from jax.experimental.pallas import tpu as pltpu
from jax.sharding import PartitionSpec as P

D = 2048
HEAD_DIM = 64
CB = 4
CACHE = 128

epsilon = 1e-05
far_below = -1e30

f32, bf16 = jnp.float32, jnp.bfloat16


def exchange(blocks, axis):
    return lax.all_to_all(blocks, axis, split_axis=0, concat_axis=0, tiled=True)


def spread_kernel(block_ref, copies_ref, sent):
    copies = [
        pltpu.make_async_copy(block_ref, copies_ref.at[k], sent.at[k])
        for k in range(copies_ref.shape[0])
    ]
    for copy in copies:
        copy.start()
    for copy in copies:
        copy.wait()


def spread(block, count):
    return pl.pallas_call(
        spread_kernel,
        out_shape=jax.ShapeDtypeStruct((count, *block.shape), block.dtype),
        in_specs=[pl.BlockSpec(memory_space=pl.ANY)],
        out_specs=pl.BlockSpec(memory_space=pl.ANY),
        scratch_shapes=[pltpu.SemaphoreType.DMA((count,))],
        compiler_params=pltpu.CompilerParams(vmem_limit_bytes=8 << 20),
    )(block)


def residual_kernel(shares_ref, hidden_ref, residual_ref, copies_ref, sent):
    total = hidden_ref[...].astype(f32) + jnp.sum(shares_ref[...], 0)
    residual_ref[...] = total.astype(bf16)
    spread_kernel(residual_ref, copies_ref, sent)


PIECES = ((0,), (1,), (4, 5), (2, 3, 6, 7), (-1, -2, -5, -6), (-3, -4, -7, -8))


def moved(array, steps):
    count = lax.axis_size("dp")
    route = []
    for target in range(count):
        source = target + steps if target % 2 else target - steps
        route.append((source % count, target))
    return lax.ppermute(array, "dp", route)


def join_kernel(*refs):
    pieces, out_ref, arrived = refs[:-2], refs[-2], refs[-1]
    copies, at = [], 0
    for k, piece in enumerate(pieces):
        target = out_ref.at[pl.ds(at, piece.shape[0])]
        copies.append(pltpu.make_async_copy(piece, target, arrived.at[k]))
        at += piece.shape[0]
    for copy in copies:
        copy.start()
    for copy in copies:
        copy.wait()


def joined(*pieces):
    rows = sum(piece.shape[0] for piece in pieces)
    return pl.pallas_call(
        join_kernel,
        out_shape=jax.ShapeDtypeStruct((rows, *pieces[0].shape[1:]), pieces[0].dtype),
        in_specs=[pl.BlockSpec(memory_space=pl.ANY)] * len(pieces),
        out_specs=pl.BlockSpec(memory_space=pl.ANY),
        scratch_shapes=[pltpu.SemaphoreType.DMA((len(pieces),))],
        compiler_params=pltpu.CompilerParams(vmem_limit_bytes=8 << 20),
    )(*pieces)


def first_heads(block):
    next_one = moved(block, 1)
    return block, next_one, moved(joined(block, next_one), 4)


def second_heads(*heads):
    held = joined(*heads)
    from_same = moved(held, 2)
    return from_same, moved(held, -1)


def third_heads(from_same):
    return moved(from_same, -1)


def normalized(rows, gain):
    count = rows.shape[0] * rows.shape[2]
    average = jnp.sum(jnp.sum(rows, 0), -1, keepdims=True) / count
    apart = rows - average[None]
    spread = jnp.sum(jnp.sum(apart * apart, 0), -1, keepdims=True) / count
    return (apart * lax.rsqrt(spread + epsilon)[None] * gain).astype(bf16)


def side_by_side(blocks):
    return jnp.concatenate(blocks, axis=-1)


def attend_kernel(
    blocks_ref,
    small_ref,
    qkv_in,
    keys_in,
    values_in,
    out_w_in,
    parts_ref,
    qkv_ref,
    keys_ref,
    values_ref,
    out_w_ref,
    arrived,
):
    count, streams, width = blocks_ref.shape
    copies = [
        pltpu.make_async_copy(source, target, arrived.at[k])
        for k, (source, target) in enumerate(
            (
                (qkv_in, qkv_ref),
                (keys_in, keys_ref),
                (values_in, values_ref),
                (out_w_in, out_w_ref),
            )
        )
    ]
    for copy in copies:
        copy.start()
    gain = small_ref[streams:][:, None, :]
    tokens = normalized(blocks_ref[...].astype(f32), gain)
    tokens = side_by_side([tokens[k] for k in range(count)])
    copies[0].wait()
    query, new_key, new_value = (
        jnp.dot(tokens, qkv_ref[slot], preferred_element_type=f32).astype(bf16).astype(f32)
        for slot in range(3)
    )
    head_of_lane = lax.broadcasted_iota(jnp.int32, (8, width), 1) // HEAD_DIM
    own_head = (head_of_lane == lax.broadcasted_iota(jnp.int32, (8, width), 0)).astype(f32)
    queries = query[:, None, :] * own_head[None]
    inv_root = 1.0 / HEAD_DIM**0.5
    copies[1].wait()
    scores = (
        lax.dot_general(
            queries.astype(bf16),
            keys_ref[...],
            (((2,), (2,)), ((0,), (0,))),
            preferred_element_type=f32,
        )
        * inv_root
    )
    scores = jnp.where(small_ref[:streams][:, None, :] > 0, scores, far_below)
    self_score = jnp.sum(queries * new_key[:, None, :], -1, keepdims=True) * inv_root
    peak = jnp.maximum(jnp.max(scores, -1, keepdims=True), self_score)
    raw = jnp.exp(scores - peak)
    self_raw = jnp.exp(self_score - peak)
    denom = jnp.sum(raw, -1, keepdims=True) + self_raw
    weights = (raw / denom).astype(bf16)
    self_weight = (self_raw / denom).astype(bf16).astype(f32)
    copies[2].wait()
    attended = lax.dot_general(
        weights, values_ref[...], (((2,), (1,)), ((0,), (0,))), preferred_element_type=f32
    )
    attended = (attended + self_weight * new_value[:, None, :]) * own_head[None]
    attended = jnp.sum(attended, 1).astype(bf16)
    copies[3].wait()
    projected = jnp.dot(attended, out_w_ref[...], preferred_element_type=f32)
    for k in range(count):
        parts_ref[k] = projected[:, k * width : (k + 1) * width]


def norm_kernel(rows_ref, gain_ref, normed_ref):
    count = gain_ref.shape[0]
    for branch in range(2):
        rows = rows_ref[branch * count : (branch + 1) * count].astype(f32)
        normed_ref[branch] = normalized(rows, gain_ref[...])


def logits_kernel(place_ref, normed_ref, guidance_ref, noise_ref, *refs):
    piece_refs, (perturbed_ref, mass_ref) = refs[: len(PIECES)], refs[len(PIECES) :]
    count = normed_ref.shape[1]
    streams = noise_ref.shape[0]
    z = place_ref[0]
    upwards = 2 * lax.rem(z, 2) - 1
    total = None
    for offsets, piece_ref in zip(PIECES, piece_refs):
        at = [lax.rem(z + k * upwards + count, count) for k in offsets]
        rows = [side_by_side([normed_ref[branch, k] for k in at]) for branch in range(2)]
        rows = jnp.concatenate(rows, 0)
        part = jnp.dot(rows, piece_ref[...], preferred_element_type=f32)
        total = part if total is None else total + part
    conditioned, unconditioned = total[:streams], total[streams:]
    guided = unconditioned + guidance_ref[...] * (conditioned - unconditioned)
    perturbed = guided + noise_ref[...]
    perturbed_ref[...] = perturbed
    width = perturbed.shape[1] // 2
    lane = lax.broadcasted_iota(jnp.int32, (width, width), 1)
    columns = jnp.zeros((width, width), f32)
    for book in range(2):
        codes = perturbed[:, book * width : (book + 1) * width]
        peak = jnp.max(codes, -1, keepdims=True)
        mass = jnp.log(jnp.sum(jnp.exp(codes - peak), -1, keepdims=True)) + peak
        mass = jnp.concatenate([mass, jnp.zeros((width - streams, 1), f32)], 0)
        columns = jnp.where(lane == book, mass, columns)
    mass = columns.T[:8]
    for k in range(count):
        mass_ref[k] = mass


def final_kernel(mass_ref, perturbed_ref, out_ref):
    streams = perturbed_ref.shape[0]
    masses = mass_ref[...]
    peak = jnp.max(masses, 0)
    total = jnp.log(jnp.sum(jnp.exp(masses - peak[None]), 0)) + peak
    width = total.shape[1]
    total = jnp.concatenate([total, jnp.zeros((width - 8, width), f32)], 0).T
    for book in range(2):
        codes = perturbed_ref[:, book * width : (book + 1) * width]
        out_ref[:, book, :] = codes - total[:streams, book : book + 1]


def vmem(count):
    return [pl.BlockSpec(memory_space=pltpu.VMEM)] * count


def body(
    hidden_in,
    attn_gain,
    w_qkv,
    w_out,
    cache_keys,
    cache_values,
    cache_len,
    text_len,
    final_gain,
    lm_head,
    guidance,
    uniforms,
):
    branch_index = lax.axis_index("cfg")
    z = lax.axis_index("dp")
    count = lax.axis_size("tp")
    streams, width = hidden_in.shape[1:]
    half_books = CB // 2
    blocks = exchange(spread(hidden_in[0], count), "tp")
    positions = jnp.arange(CACHE, dtype=jnp.int32)
    usable = (positions[None, :] < cache_len[:, None]) & (
        (branch_index == 0) | (positions[None, :] >= text_len[:, None])
    )
    small = jnp.concatenate([usable.astype(f32), attn_gain.reshape(count, width)], 0)
    head_half = lax.dynamic_slice_in_dim(lm_head, branch_index * half_books, half_books, 0)
    heads = first_heads(jnp.moveaxis(head_half, 0, 1).reshape(lm_head.shape[1], -1))
    noise = -jnp.log(-jnp.log(uniforms)).reshape(streams, half_books * width)
    parts = pl.pallas_call(
        attend_kernel,
        out_shape=jax.ShapeDtypeStruct((count, streams, width), f32),
        in_specs=vmem(2) + [pl.BlockSpec(memory_space=pltpu.HBM)] * 4,
        out_specs=pl.BlockSpec(memory_space=pltpu.VMEM),
        scratch_shapes=[
            pltpu.VMEM((3, D, width), bf16),
            pltpu.VMEM(cache_keys.shape[1:], bf16),
            pltpu.VMEM(cache_values.shape[1:], bf16),
            pltpu.VMEM(w_out.shape, bf16),
            pltpu.SemaphoreType.DMA((4,)),
        ],
        compiler_params=pltpu.CompilerParams(vmem_limit_bytes=54600 << 10),
        cost_estimate=pl.CostEstimate(flops=2 * 10**11, bytes_accessed=50 << 20, transcendentals=10**5),
    )(
        blocks,
        small,
        jnp.moveaxis(w_qkv, 1, 0),
        cache_keys[0],
        cache_values[0],
        w_out,
    )
    parts, heads = lax.optimization_barrier((parts, heads))
    shares = exchange(parts, "tp")
    heads += second_heads(*heads)
    everywhere = 2 * count
    residual_part, copies = pl.pallas_call(
        residual_kernel,
        out_shape=(
            jax.ShapeDtypeStruct((streams, width), bf16),
            jax.ShapeDtypeStruct((everywhere, streams, width), bf16),
        ),
        in_specs=vmem(2),
        out_specs=(vmem(1)[0], pl.BlockSpec(memory_space=pl.ANY)),
        scratch_shapes=[pltpu.SemaphoreType.DMA((everywhere,))],
        compiler_params=pltpu.CompilerParams(vmem_limit_bytes=8 << 20),
    )(shares, hidden_in[0])
    rows = exchange(copies, ("cfg", "tp"))
    from_same, swap = lax.optimization_barrier(heads[3:])
    heads = heads[:3] + (from_same, swap, third_heads(from_same))
    normed = pl.pallas_call(
        norm_kernel,
        out_shape=jax.ShapeDtypeStruct((2, count, streams, width), bf16),
        in_specs=vmem(2),
        out_specs=vmem(1)[0],
        compiler_params=pltpu.CompilerParams(vmem_limit_bytes=8 << 20),
        cost_estimate=pl.CostEstimate(flops=2 * 10**10, bytes_accessed=50 << 20, transcendentals=64),
    )(rows, final_gain.reshape(count, 1, width))
    perturbed, mass = pl.pallas_call(
        logits_kernel,
        out_shape=(
            jax.ShapeDtypeStruct((streams, half_books * width), f32),
            jax.ShapeDtypeStruct((count, 8, width), f32),
        ),
        in_specs=[pl.BlockSpec(memory_space=pltpu.SMEM)] + vmem(3 + len(heads)),
        out_specs=tuple(vmem(2)),
        compiler_params=pltpu.CompilerParams(vmem_limit_bytes=8 << 20),
        cost_estimate=pl.CostEstimate(flops=10**8, bytes_accessed=2 << 20, transcendentals=10**4),
    )(
        z[None].astype(jnp.int32),
        normed,
        guidance[:, None],
        noise,
        *heads,
    )
    masses = exchange(mass, "tp")
    sample_logprobs = pl.pallas_call(
        final_kernel,
        out_shape=jax.ShapeDtypeStruct((streams, half_books, width), f32),
        in_specs=vmem(2),
        out_specs=pl.BlockSpec(memory_space=pltpu.VMEM),
        compiler_params=pltpu.CompilerParams(vmem_limit_bytes=8 << 20),
    )(masses, perturbed)
    return (sample_logprobs, residual_part[None])


def solution(mesh):
    placed = (
        P("cfg", "dp", "tp"),
        P(),
        P(None, None, "tp"),
        P("tp", None),
        P("cfg", "dp", None, "tp"),
        P("cfg", "dp", None, "tp"),
        P("dp"),
        P("dp"),
        P(),
        P(None, "dp", "tp"),
        P("dp"),
        P("dp", "cfg", "tp"),
    )
    return jax.shard_map(
        body,
        mesh=mesh,
        in_specs=placed,
        out_specs=(P("dp", "cfg", "tp"), P("cfg", "dp", "tp")),
        check_vma=False,
    )
```

```python
import jax
import jax.numpy as jnp
from jax import lax
from jax.experimental import pallas as pl
from jax.experimental.pallas import tpu as pltpu
from jax.sharding import PartitionSpec as P

D = 2048
HEAD_DIM = 64
CB = 4
CACHE = 128

epsilon = 1e-05
far_below = -1e30

f32, bf16 = jnp.float32, jnp.bfloat16


def exchange(blocks, axis):
    return lax.all_to_all(blocks, axis, split_axis=0, concat_axis=0, tiled=True)


def spread_kernel(block_ref, copies_ref, sent):
    copies = [
        pltpu.make_async_copy(block_ref, copies_ref.at[k], sent.at[k])
        for k in range(copies_ref.shape[0])
    ]
    for copy in copies:
        copy.start()
    for copy in copies:
        copy.wait()


def spread(block, count):
    return pl.pallas_call(
        spread_kernel,
        out_shape=jax.ShapeDtypeStruct((count, *block.shape), block.dtype),
        in_specs=[pl.BlockSpec(memory_space=pl.ANY)],
        out_specs=pl.BlockSpec(memory_space=pl.ANY),
        scratch_shapes=[pltpu.SemaphoreType.DMA((count,))],
        compiler_params=pltpu.CompilerParams(vmem_limit_bytes=60 << 20),
        cost_estimate=pl.CostEstimate(flops=2*10**11, bytes_accessed=1 << 20, transcendentals=0),
    )(block)


PIECES = ((0, 1, 4, 5), (2, 3, 6, 7), (-1, -2, -5, -6), (-3, -4, -7, -8))


def moved(array, steps):
    count = lax.axis_size("dp")
    route = []
    for target in range(count):
        source = target + steps if target % 2 else target - steps
        route.append((source % count, target))
    return lax.ppermute(array, "dp", route)


def join_kernel(*refs):
    pieces, out_ref, arrived = refs[:-2], refs[-2], refs[-1]
    copies, at = [], 0
    for k, piece in enumerate(pieces):
        target = out_ref.at[pl.ds(at, piece.shape[0])]
        copies.append(pltpu.make_async_copy(piece, target, arrived.at[k]))
        at += piece.shape[0]
    for copy in copies:
        copy.start()
    for copy in copies:
        copy.wait()


def joined(*pieces):
    rows = sum(piece.shape[0] for piece in pieces)
    return pl.pallas_call(
        join_kernel,
        out_shape=jax.ShapeDtypeStruct((rows, *pieces[0].shape[1:]), pieces[0].dtype),
        in_specs=[pl.BlockSpec(memory_space=pl.ANY)] * len(pieces),
        out_specs=pl.BlockSpec(memory_space=pl.ANY),
        scratch_shapes=[pltpu.SemaphoreType.DMA((len(pieces),))],
        compiler_params=pltpu.CompilerParams(vmem_limit_bytes=8 << 20),
        cost_estimate=pl.CostEstimate(flops=2*10**10, bytes_accessed=1 << 20, transcendentals=0),
    )(*pieces)


def first_heads(block):
    next_one = moved(block, 1)
    return block, next_one, moved(joined(block, next_one), 4)


def second_heads(*heads):
    held = joined(*heads)
    from_same = moved(held, 2)
    return held, from_same, moved(held, -1)


def third_heads(from_same):
    return moved(from_same, -1)


def normalized(rows, gain):
    count = rows.shape[0] * rows.shape[2]
    average = jnp.sum(jnp.sum(rows, 0), -1, keepdims=True) / count
    apart = rows - average[None]
    spread = jnp.sum(jnp.sum(apart * apart, 0), -1, keepdims=True) / count
    return (apart * lax.rsqrt(spread + epsilon)[None] * gain).astype(bf16)


def side_by_side(blocks):
    return jnp.concatenate(blocks, axis=-1)


def attend_kernel(
    blocks_ref,
    small_ref,
    keys_ref,
    values_ref,
    out_w_ref,
    qkv_in,
    parts_ref,
    qkv_ref,
    arrived,
):
    count, streams, width = blocks_ref.shape
    copies = [
        pltpu.make_async_copy(qkv_in.at[slot], qkv_ref.at[slot], arrived.at[slot])
        for slot in range(3)
    ]
    for copy in copies:
        copy.start()
    gain = small_ref[streams:][:, None, :]
    tokens = normalized(blocks_ref[...].astype(f32), gain)
    tokens = side_by_side([tokens[k] for k in range(count)])
    projections = []
    for slot in range(3):
        copies[slot].wait()
        slot_rows = jnp.dot(tokens, qkv_ref[slot], preferred_element_type=f32)
        projections.append(slot_rows.astype(bf16).astype(f32))
    query, new_key, new_value = projections
    head_of_lane = lax.broadcasted_iota(jnp.int32, (8, width), 1) // HEAD_DIM
    own_head = (head_of_lane == lax.broadcasted_iota(jnp.int32, (8, width), 0)).astype(f32)
    queries = query[:, None, :] * own_head[None]
    inv_root = 1.0 / HEAD_DIM**0.5
    scores = (
        lax.dot_general(
            queries.astype(bf16),
            keys_ref[...],
            (((2,), (2,)), ((0,), (0,))),
            preferred_element_type=f32,
        )
        * inv_root
    )
    scores = jnp.where(small_ref[:streams][:, None, :] > 0, scores, far_below)
    self_score = jnp.sum(queries * new_key[:, None, :], -1, keepdims=True) * inv_root
    peak = jnp.maximum(jnp.max(scores, -1, keepdims=True), self_score)
    raw = jnp.exp(scores - peak)
    self_raw = jnp.exp(self_score - peak)
    denom = jnp.sum(raw, -1, keepdims=True) + self_raw
    weights = (raw / denom).astype(bf16)
    self_weight = (self_raw / denom).astype(bf16).astype(f32)
    attended = lax.dot_general(
        weights, values_ref[...], (((2,), (1,)), ((0,), (0,))), preferred_element_type=f32
    )
    attended = (attended + self_weight * new_value[:, None, :]) * own_head[None]
    attended = jnp.sum(attended, 1).astype(bf16)
    projected = jnp.dot(attended, out_w_ref[...], preferred_element_type=f32)
    for k in range(count):
        parts_ref[k] = projected[:, k * width : (k + 1) * width]


def partial_logits(z, normed_ref, pieces, piece_refs):
    count = normed_ref.shape[1]
    upwards = 2 * lax.rem(z, 2) - 1
    total = None
    for offsets, piece_ref in zip(pieces, piece_refs):
        at = [lax.rem(z + k * upwards + count, count) for k in offsets]
        rows = [side_by_side([normed_ref[branch, k] for k in at]) for branch in range(2)]
        rows = jnp.concatenate(rows, 0)
        part = jnp.dot(rows, piece_ref[...], preferred_element_type=f32)
        total = part if total is None else total + part
    return total


def norm_kernel(place_ref, rows_ref, gain_ref, *refs):
    piece_refs, (normed_ref, part_ref) = refs[:-2], refs[-2:]
    count = gain_ref.shape[0]
    for branch in range(2):
        rows = rows_ref[branch * count : (branch + 1) * count].astype(f32)
        normed_ref[branch] = normalized(rows, gain_ref[...])
    part_ref[...] = partial_logits(place_ref[0], normed_ref, PIECES[:-1], piece_refs)


def logits_kernel(
    place_ref, normed_ref, part_ref, guidance_ref, noise_ref, piece_ref, perturbed_ref, mass_ref
):
    count = normed_ref.shape[1]
    streams = noise_ref.shape[0]
    total = part_ref[...] + partial_logits(place_ref[0], normed_ref, PIECES[-1:], [piece_ref])
    conditioned, unconditioned = total[:streams], total[streams:]
    guided = unconditioned + guidance_ref[...] * (conditioned - unconditioned)
    perturbed = guided + noise_ref[...]
    perturbed_ref[...] = perturbed
    width = perturbed.shape[1] // 2
    lane = lax.broadcasted_iota(jnp.int32, (width, width), 1)
    columns = jnp.zeros((width, width), f32)
    for book in range(2):
        codes = perturbed[:, book * width : (book + 1) * width]
        peak = jnp.max(codes, -1, keepdims=True)
        mass = jnp.log(jnp.sum(jnp.exp(codes - peak), -1, keepdims=True)) + peak
        mass = jnp.concatenate([mass, jnp.zeros((width - streams, 1), f32)], 0)
        columns = jnp.where(lane == book, mass, columns)
    mass = columns.T[:8]
    for k in range(count):
        mass_ref[k] = mass


def final_kernel(mass_ref, perturbed_ref, out_ref):
    streams = perturbed_ref.shape[0]
    masses = mass_ref[...]
    peak = jnp.max(masses, 0)
    total = jnp.log(jnp.sum(jnp.exp(masses - peak[None]), 0)) + peak
    width = total.shape[1]
    total = jnp.concatenate([total, jnp.zeros((width - 8, width), f32)], 0).T
    for book in range(2):
        codes = perturbed_ref[:, book * width : (book + 1) * width]
        out_ref[:, book, :] = codes - total[:streams, book : book + 1]


def vmem(count):
    return [pl.BlockSpec(memory_space=pltpu.VMEM)] * count


def body(
    hidden_in,
    attn_gain,
    w_qkv,
    w_out,
    cache_keys,
    cache_values,
    cache_len,
    text_len,
    final_gain,
    lm_head,
    guidance,
    uniforms,
):
    branch_index = lax.axis_index("cfg")
    z = lax.axis_index("dp")
    count = lax.axis_size("tp")
    streams, width = hidden_in.shape[1:]
    half_books = CB // 2
    blocks = exchange(spread(hidden_in[0], count), "tp")
    positions = jnp.arange(CACHE, dtype=jnp.int32)
    usable = (positions[None, :] < cache_len[:, None]) & (
        (branch_index == 0) | (positions[None, :] >= text_len[:, None])
    )
    small = jnp.concatenate([usable.astype(f32), attn_gain.reshape(count, width)], 0)
    head_half = lax.dynamic_slice_in_dim(lm_head, branch_index * half_books, half_books, 0)
    heads = first_heads(jnp.moveaxis(head_half, 0, 1).reshape(lm_head.shape[1], -1))
    noise = -jnp.log(-jnp.log(uniforms)).reshape(streams, half_books * width)
    parts = pl.pallas_call(
        attend_kernel,
        out_shape=jax.ShapeDtypeStruct((count, streams, width), f32),
        in_specs=vmem(5) + [pl.BlockSpec(memory_space=pltpu.HBM)],
        out_specs=vmem(1)[0],
        scratch_shapes=[pltpu.VMEM((3, D, width), bf16), pltpu.SemaphoreType.DMA((3,))],
        compiler_params=pltpu.CompilerParams(vmem_limit_bytes=51456 << 10),
        cost_estimate=pl.CostEstimate(flops=2 * 10**11, bytes_accessed=50 << 20, transcendentals=10**5),
    )(
        blocks,
        small,
        cache_keys[0],
        cache_values[0],
        w_out,
        jnp.moveaxis(w_qkv, 1, 0),
    )
    parts, heads = lax.optimization_barrier((parts, heads))
    shares = exchange(parts, "tp")
    held, from_same, swap = second_heads(*heads)
    residual_part = (hidden_in[0].astype(f32) + shares.sum(0)).astype(bf16)
    copies = jnp.broadcast_to(residual_part, (2 * count, streams, width))
    rows = exchange(copies, ("cfg", "tp"))
    from_same, swap = lax.optimization_barrier((from_same, swap))
    heads = (held, from_same, swap, third_heads(from_same))
    place = z[None].astype(jnp.int32)
    smem = [pl.BlockSpec(memory_space=pltpu.SMEM)]
    normed, part = pl.pallas_call(
        norm_kernel,
        out_shape=(
            jax.ShapeDtypeStruct((2, count, streams, width), bf16),
            jax.ShapeDtypeStruct((2 * streams, half_books * width), f32),
        ),
        in_specs=smem + vmem(1 + len(heads)),
        out_specs=tuple(vmem(2)),
        compiler_params=pltpu.CompilerParams(vmem_limit_bytes=8 << 20),
        cost_estimate=pl.CostEstimate(flops=2 * 10**10, bytes_accessed=50 << 20, transcendentals=64),
    )(place, rows, final_gain.reshape(count, 1, width), *heads[:-1])
    perturbed, mass = pl.pallas_call(
        logits_kernel,
        out_shape=(
            jax.ShapeDtypeStruct((streams, half_books * width), f32),
            jax.ShapeDtypeStruct((count, 8, width), f32),
        ),
        in_specs=smem + vmem(5),
        out_specs=tuple(vmem(2)),
        compiler_params=pltpu.CompilerParams(vmem_limit_bytes=8 << 20),
        cost_estimate=pl.CostEstimate(flops=10**8, bytes_accessed=2 << 20, transcendentals=10**4),
    )(place, normed, part, guidance[:, None], noise, heads[-1])
    masses = exchange(mass, "tp")
    sample_logprobs = pl.pallas_call(
        final_kernel,
        out_shape=jax.ShapeDtypeStruct((streams, half_books, width), f32),
        in_specs=vmem(2),
        out_specs=pl.BlockSpec(memory_space=pltpu.VMEM),
        compiler_params=pltpu.CompilerParams(vmem_limit_bytes=8 << 20),
    )(masses, perturbed)
    return (sample_logprobs, residual_part[None])


def solution(mesh):
    placed = (
        P("cfg", "dp", "tp"),
        P(),
        P(None, None, "tp"),
        P("tp", None),
        P("cfg", "dp", None, "tp"),
        P("cfg", "dp", None, "tp"),
        P("dp"),
        P("dp"),
        P(),
        P(None, "dp", "tp"),
        P("dp"),
        P("dp", "cfg", "tp"),
    )
    return jax.shard_map(
        body,
        mesh=mesh,
        in_specs=placed,
        out_specs=(P("dp", "cfg", "tp"), P("cfg", "dp", "tp")),
        check_vma=False,
    )
```

```python
import jax
import jax.numpy as jnp
from jax import lax
from jax.experimental import pallas as pl
from jax.experimental.pallas import tpu as pltpu
from jax.sharding import PartitionSpec as P

D = 2048
HEAD_DIM = 64
CB = 4
CACHE = 128

epsilon = 1e-05
far_below = -1e30

f32, bf16 = jnp.float32, jnp.bfloat16


def exchange(blocks, axis):
    return lax.all_to_all(blocks, axis, split_axis=0, concat_axis=0, tiled=True)


def spread_kernel(block_ref, copies_ref, held_ref, sent):
    count = copies_ref.shape[0]
    copy = pltpu.make_async_copy(block_ref, held_ref, sent.at[count])
    copy.start()
    copy.wait()
    copies = [
        pltpu.make_async_copy(held_ref, copies_ref.at[k], sent.at[k]) for k in range(count)
    ]
    for copy in copies:
        copy.start()
    for copy in copies:
        copy.wait()


def spread(block, count):
    return pl.pallas_call(
        spread_kernel,
        out_shape=jax.ShapeDtypeStruct((count, *block.shape), block.dtype),
        in_specs=[pl.BlockSpec(memory_space=pl.ANY)],
        out_specs=pl.BlockSpec(memory_space=pl.ANY),
        scratch_shapes=[
            pltpu.VMEM(block.shape, block.dtype),
            pltpu.SemaphoreType.DMA((count + 1,)),
        ],
        compiler_params=pltpu.CompilerParams(vmem_limit_bytes=60 << 20),
        cost_estimate=pl.CostEstimate(flops=2 * 10**11, bytes_accessed=1 << 20, transcendentals=0),
    )(block)


PIECES = ((0, 1, 4, 5), (2, 3, 6, 7), (-1, -2, -5, -6), (-3, -4, -7, -8))


def moved(array, steps):
    count = lax.axis_size("dp")
    route = []
    for target in range(count):
        source = target + steps if target % 2 else target - steps
        route.append((source % count, target))
    return lax.ppermute(array, "dp", route)


def join_kernel(*refs):
    pieces, out_ref, arrived = refs[:-2], refs[-2], refs[-1]
    copies, at = [], 0
    for k, piece in enumerate(pieces):
        target = out_ref.at[pl.ds(at, piece.shape[0])]
        copies.append(pltpu.make_async_copy(piece, target, arrived.at[k]))
        at += piece.shape[0]
    for copy in copies:
        copy.start()
    for copy in copies:
        copy.wait()


def joined(*pieces):
    rows = sum(piece.shape[0] for piece in pieces)
    return pl.pallas_call(
        join_kernel,
        out_shape=jax.ShapeDtypeStruct((rows, *pieces[0].shape[1:]), pieces[0].dtype),
        in_specs=[pl.BlockSpec(memory_space=pl.ANY)] * len(pieces),
        out_specs=vmem(1)[0],
        scratch_shapes=[pltpu.SemaphoreType.DMA((len(pieces),))],
        compiler_params=pltpu.CompilerParams(vmem_limit_bytes=8 << 20),
        cost_estimate=pl.CostEstimate(flops=2 * 10**10, bytes_accessed=1 << 20, transcendentals=0),
    )(*pieces)


def first_heads(block):
    next_one = moved(block, 1)
    return block, next_one, moved(joined(block, next_one), 4)


def second_heads(*heads):
    held = joined(*heads)
    from_same = moved(held, 2)
    return held, from_same, moved(held, -1)


def third_heads(from_same):
    return moved(from_same, -1)


def normalized(rows, gain):
    count = rows.shape[0] * rows.shape[2]
    average = jnp.sum(jnp.sum(rows, 0), -1, keepdims=True) / count
    apart = rows - average[None]
    spread = jnp.sum(jnp.sum(apart * apart, 0), -1, keepdims=True) / count
    return (apart * lax.rsqrt(spread + epsilon)[None] * gain).astype(bf16)


def side_by_side(blocks):
    return jnp.concatenate(blocks, axis=-1)


def attend_kernel(
    blocks_ref,
    small_ref,
    keys_ref,
    values_ref,
    out_w_ref,
    qkv_in,
    parts_ref,
    qkv_ref,
    arrived,
):
    count, streams, width = blocks_ref.shape
    copies = [
        pltpu.make_async_copy(qkv_in.at[slot], qkv_ref.at[slot], arrived.at[slot])
        for slot in range(3)
    ]
    for copy in copies:
        copy.start()
    gain = small_ref[streams:][:, None, :]
    tokens = normalized(blocks_ref[...].astype(f32), gain)
    tokens = side_by_side([tokens[k] for k in range(count)])
    projections = []
    for slot in range(3):
        copies[slot].wait()
        slot_rows = jnp.dot(tokens, qkv_ref[slot], preferred_element_type=f32)
        projections.append(slot_rows.astype(bf16).astype(f32))
    query, new_key, new_value = projections
    head_of_lane = lax.broadcasted_iota(jnp.int32, (8, width), 1) // HEAD_DIM
    own_head = (head_of_lane == lax.broadcasted_iota(jnp.int32, (8, width), 0)).astype(f32)
    queries = query[:, None, :] * own_head[None]
    inv_root = 1.0 / HEAD_DIM**0.5
    scores = (
        lax.dot_general(
            queries.astype(bf16),
            keys_ref[...],
            (((2,), (2,)), ((0,), (0,))),
            preferred_element_type=f32,
        )
        * inv_root
    )
    scores = jnp.where(small_ref[:streams][:, None, :] > 0, scores, far_below)
    self_score = jnp.sum(queries * new_key[:, None, :], -1, keepdims=True) * inv_root
    peak = jnp.maximum(jnp.max(scores, -1, keepdims=True), self_score)
    raw = jnp.exp(scores - peak)
    self_raw = jnp.exp(self_score - peak)
    denom = jnp.sum(raw, -1, keepdims=True) + self_raw
    weights = (raw / denom).astype(bf16)
    self_weight = (self_raw / denom).astype(bf16).astype(f32)
    attended = lax.dot_general(
        weights, values_ref[...], (((2,), (1,)), ((0,), (0,))), preferred_element_type=f32
    )
    attended = (attended + self_weight * new_value[:, None, :]) * own_head[None]
    attended = jnp.sum(attended, 1).astype(bf16)
    projected = jnp.dot(attended, out_w_ref[...], preferred_element_type=f32)
    for k in range(count):
        parts_ref[k] = projected[:, k * width : (k + 1) * width]


def partial_logits(z, normed_ref, pieces, piece_refs):
    count = normed_ref.shape[1]
    upwards = 2 * lax.rem(z, 2) - 1
    total = None
    for offsets, piece_ref in zip(pieces, piece_refs):
        at = [lax.rem(z + k * upwards + count, count) for k in offsets]
        rows = [side_by_side([normed_ref[branch, k] for k in at]) for branch in range(2)]
        rows = jnp.concatenate(rows, 0)
        part = jnp.dot(rows, piece_ref[...], preferred_element_type=f32)
        total = part if total is None else total + part
    return total


def norm_kernel(place_ref, rows_ref, gain_ref, *refs):
    piece_refs, (normed_ref, part_ref) = refs[:-2], refs[-2:]
    count = gain_ref.shape[0]
    for branch in range(2):
        rows = rows_ref[branch * count : (branch + 1) * count].astype(f32)
        normed_ref[branch] = normalized(rows, gain_ref[...])
    part_ref[...] = partial_logits(place_ref[0], normed_ref, PIECES[:-1], piece_refs)


def logits_kernel(
    place_ref, normed_ref, part_ref, guidance_ref, noise_ref, piece_ref, perturbed_ref, mass_ref
):
    count = normed_ref.shape[1]
    streams = noise_ref.shape[0]
    total = part_ref[...] + partial_logits(place_ref[0], normed_ref, PIECES[-1:], [piece_ref])
    conditioned, unconditioned = total[:streams], total[streams:]
    guided = unconditioned + guidance_ref[...] * (conditioned - unconditioned)
    perturbed = guided + noise_ref[...]
    perturbed_ref[...] = perturbed
    width = perturbed.shape[1] // 2
    lane = lax.broadcasted_iota(jnp.int32, (width, width), 1)
    columns = jnp.zeros((width, width), f32)
    for book in range(2):
        codes = perturbed[:, book * width : (book + 1) * width]
        peak = jnp.max(codes, -1, keepdims=True)
        mass = jnp.log(jnp.sum(jnp.exp(codes - peak), -1, keepdims=True)) + peak
        mass = jnp.concatenate([mass, jnp.zeros((width - streams, 1), f32)], 0)
        columns = jnp.where(lane == book, mass, columns)
    mass = columns.T[:8]
    for k in range(count):
        mass_ref[k] = mass


def final_kernel(mass_ref, perturbed_ref, out_ref):
    streams = perturbed_ref.shape[0]
    masses = mass_ref[...]
    peak = jnp.max(masses, 0)
    total = jnp.log(jnp.sum(jnp.exp(masses - peak[None]), 0)) + peak
    width = total.shape[1]
    total = jnp.concatenate([total, jnp.zeros((width - 8, width), f32)], 0).T
    for book in range(2):
        codes = perturbed_ref[:, book * width : (book + 1) * width]
        out_ref[:, book, :] = codes - total[:streams, book : book + 1]


def vmem(count):
    return [pl.BlockSpec(memory_space=pltpu.VMEM)] * count


def body(
    hidden_in,
    attn_gain,
    w_qkv,
    w_out,
    cache_keys,
    cache_values,
    cache_len,
    text_len,
    final_gain,
    lm_head,
    guidance,
    uniforms,
):
    branch_index = lax.axis_index("cfg")
    z = lax.axis_index("dp")
    count = lax.axis_size("tp")
    streams, width = hidden_in.shape[1:]
    half_books = CB // 2
    blocks = exchange(spread(hidden_in[0], count), "tp")
    positions = jnp.arange(CACHE, dtype=jnp.int32)
    usable = (positions[None, :] < cache_len[:, None]) & (
        (branch_index == 0) | (positions[None, :] >= text_len[:, None])
    )
    small = jnp.concatenate([usable.astype(f32), attn_gain.reshape(count, width)], 0)
    head_half = lax.dynamic_slice_in_dim(lm_head, branch_index * half_books, half_books, 0)
    heads = first_heads(jnp.moveaxis(head_half, 0, 1).reshape(lm_head.shape[1], -1))
    noise = -jnp.log(-jnp.log(uniforms)).reshape(streams, half_books * width)
    parts = pl.pallas_call(
        attend_kernel,
        out_shape=jax.ShapeDtypeStruct((count, streams, width), f32),
        in_specs=vmem(5) + [pl.BlockSpec(memory_space=pltpu.HBM)],
        out_specs=vmem(1)[0],
        scratch_shapes=[pltpu.VMEM((3, D, width), bf16), pltpu.SemaphoreType.DMA((3,))],
        compiler_params=pltpu.CompilerParams(vmem_limit_bytes=51456 << 10),
        cost_estimate=pl.CostEstimate(flops=2 * 10**11, bytes_accessed=50 << 20, transcendentals=10**5),
    )(
        blocks,
        small,
        cache_keys[0],
        cache_values[0],
        w_out,
        jnp.moveaxis(w_qkv, 1, 0),
    )
    shares = exchange(parts, "tp")
    held, from_same, swap = second_heads(*heads)
    residual_part = (hidden_in[0].astype(f32) + shares.sum(0)).astype(bf16)
    copies = jnp.broadcast_to(residual_part, (2 * count, streams, width))
    rows = exchange(copies, ("cfg", "tp"))
    from_same, swap = lax.optimization_barrier((from_same, swap))
    heads = (held, from_same, swap, third_heads(from_same))
    place = z[None].astype(jnp.int32)
    smem = [pl.BlockSpec(memory_space=pltpu.SMEM)]
    normed, part = pl.pallas_call(
        norm_kernel,
        out_shape=(
            jax.ShapeDtypeStruct((2, count, streams, width), bf16),
            jax.ShapeDtypeStruct((2 * streams, half_books * width), f32),
        ),
        in_specs=smem + vmem(1 + len(heads)),
        out_specs=tuple(vmem(2)),
        compiler_params=pltpu.CompilerParams(vmem_limit_bytes=8 << 20),
        cost_estimate=pl.CostEstimate(flops=2 * 10**10, bytes_accessed=50 << 20, transcendentals=64),
    )(place, rows, final_gain.reshape(count, 1, width), *heads[:-1])
    perturbed, mass = pl.pallas_call(
        logits_kernel,
        out_shape=(
            jax.ShapeDtypeStruct((streams, half_books * width), f32),
            jax.ShapeDtypeStruct((count, 8, width), f32),
        ),
        in_specs=smem + vmem(5),
        out_specs=tuple(vmem(2)),
        compiler_params=pltpu.CompilerParams(vmem_limit_bytes=8 << 20),
        cost_estimate=pl.CostEstimate(flops=10**8, bytes_accessed=2 << 20, transcendentals=10**4),
    )(place, normed, part, guidance[:, None], noise, heads[-1])
    masses = exchange(mass, "tp")
    sample_logprobs = pl.pallas_call(
        final_kernel,
        out_shape=jax.ShapeDtypeStruct((streams, half_books, width), f32),
        in_specs=vmem(2),
        out_specs=pl.BlockSpec(memory_space=pltpu.VMEM),
        compiler_params=pltpu.CompilerParams(vmem_limit_bytes=8 << 20),
    )(masses, perturbed)
    return (sample_logprobs, residual_part[None])


def solution(mesh):
    placed = (
        P("cfg", "dp", "tp"),
        P(),
        P(None, None, "tp"),
        P("tp", None),
        P("cfg", "dp", None, "tp"),
        P("cfg", "dp", None, "tp"),
        P("dp"),
        P("dp"),
        P(),
        P(None, "dp", "tp"),
        P("dp"),
        P("dp", "cfg", "tp"),
    )
    return jax.shard_map(
        body,
        mesh=mesh,
        in_specs=placed,
        out_specs=(P("dp", "cfg", "tp"), P("cfg", "dp", "tp")),
        check_vma=False,
    )
```

```python
import jax
import jax.numpy as jnp
from jax import lax
from jax.experimental import pallas as pl
from jax.experimental.pallas import tpu as pltpu
from jax.sharding import PartitionSpec as P

D = 2048
HEAD_DIM = 64
CB = 4
CACHE = 128

epsilon = 1e-05
far_below = -1e30

f32, bf16 = jnp.float32, jnp.bfloat16


def exchange(blocks, axis):
    return lax.all_to_all(blocks, axis, split_axis=0, concat_axis=0, tiled=True)


def start_kernel(hidden_ref, head_ref, block_ref, copies_ref, sent):
    count = copies_ref.shape[0]
    width = head_ref.shape[2]
    books = head_ref.shape[0] // 2
    branch = lax.axis_index("cfg")
    heads = [
        pltpu.make_async_copy(
            head_ref.at[branch * books + book],
            block_ref.at[:, pl.ds(book * width, width)],
            sent.at[count + book],
        )
        for book in range(books)
    ]
    copies = [
        pltpu.make_async_copy(hidden_ref, copies_ref.at[k], sent.at[k]) for k in range(count)
    ]
    for copy in heads + copies:
        copy.start()
    for copy in heads + copies:
        copy.wait()


def started(hidden, lm_head, count):
    books, features, width = lm_head.shape
    return pl.pallas_call(
        start_kernel,
        out_shape=(
            jax.ShapeDtypeStruct((features, books // 2 * width), lm_head.dtype),
            jax.ShapeDtypeStruct((count, *hidden.shape), hidden.dtype),
        ),
        in_specs=vmem(1) + [pl.BlockSpec(memory_space=pl.ANY)],
        out_specs=(vmem(1)[0], pl.BlockSpec(memory_space=pl.ANY)),
        scratch_shapes=[pltpu.SemaphoreType.DMA((count + books // 2,))],
        compiler_params=pltpu.CompilerParams(vmem_limit_bytes=55150 << 10),
        cost_estimate=pl.CostEstimate(flops=2 * 10**11, bytes_accessed=1 << 20, transcendentals=0),
    )(hidden, lm_head)


PIECES = ((0, 1, 4, 5), (2, 3, 6, 7), (-1, -2, -5, -6), (-3, -4, -7, -8))


def moved(array, steps):
    count = lax.axis_size("dp")
    route = []
    for target in range(count):
        source = target + steps if target % 2 else target - steps
        route.append((source % count, target))
    return lax.ppermute(array, "dp", route)


def join_kernel(*refs):
    pieces, out_ref, arrived = refs[:-2], refs[-2], refs[-1]
    copies, at = [], 0
    for k, piece in enumerate(pieces):
        target = out_ref.at[pl.ds(at, piece.shape[0])]
        copies.append(pltpu.make_async_copy(piece, target, arrived.at[k]))
        at += piece.shape[0]
    for copy in copies:
        copy.start()
    for copy in copies:
        copy.wait()


def joined(*pieces):
    rows = sum(piece.shape[0] for piece in pieces)
    return pl.pallas_call(
        join_kernel,
        out_shape=jax.ShapeDtypeStruct((rows, *pieces[0].shape[1:]), pieces[0].dtype),
        in_specs=[pl.BlockSpec(memory_space=pl.ANY)] * len(pieces),
        out_specs=vmem(1)[0],
        scratch_shapes=[pltpu.SemaphoreType.DMA((len(pieces),))],
        compiler_params=pltpu.CompilerParams(vmem_limit_bytes=8192 << 10),
        cost_estimate=pl.CostEstimate(flops=2 * 10**10, bytes_accessed=1 << 20, transcendentals=0),
    )(*pieces)


def first_heads(block):
    near = joined(block, moved(block, 1))
    return near, moved(near, 4)


def second_heads(near, far):
    held = joined(near, far)
    from_same = moved(held, 2)
    return held, from_same, moved(held, -1)


def third_heads(from_same):
    return moved(from_same, -1)


def normalized(rows, gain):
    count = rows.shape[0] * rows.shape[2]
    average = jnp.sum(jnp.sum(rows, 0), -1, keepdims=True) / count
    apart = rows - average[None]
    spread = jnp.sum(jnp.sum(apart * apart, 0), -1, keepdims=True) / count
    return (apart * lax.rsqrt(spread + epsilon)[None] * gain).astype(bf16)


def side_by_side(blocks):
    return jnp.concatenate(blocks, axis=-1)


def attend_kernel(
    blocks_ref,
    small_ref,
    keys_ref,
    values_ref,
    out_w_ref,
    qkv_in,
    parts_ref,
    qkv_ref,
    held_ref,
    arrived,
):
    count, streams, width = blocks_ref.shape
    copies = [
        pltpu.make_async_copy(qkv_in.at[slot], qkv_ref.at[slot], arrived.at[slot])
        for slot in range(3)
    ]
    for copy in copies:
        copy.start()
    gain = small_ref[streams:][:, None, :]
    tokens = normalized(blocks_ref[...].astype(f32), gain)
    tokens = side_by_side([tokens[k] for k in range(count)])
    projections = []
    for slot in range(3):
        copies[slot].wait()
        slot_rows = jnp.dot(tokens, qkv_ref[slot], preferred_element_type=f32)
        projections.append(slot_rows.astype(bf16).astype(f32))
    query, new_key, new_value = projections
    head_of_lane = lax.broadcasted_iota(jnp.int32, (8, width), 1) // HEAD_DIM
    own_head = (head_of_lane == lax.broadcasted_iota(jnp.int32, (8, width), 0)).astype(f32)
    queries = query[:, None, :] * own_head[None]
    inv_root = 1.0 / HEAD_DIM**0.5
    scores = (
        lax.dot_general(
            queries.astype(bf16),
            keys_ref[...],
            (((2,), (2,)), ((0,), (0,))),
            preferred_element_type=f32,
        )
        * inv_root
    )
    scores = jnp.where(small_ref[:streams][:, None, :] > 0, scores, far_below)
    self_score = jnp.sum(queries * new_key[:, None, :], -1, keepdims=True) * inv_root
    peak = jnp.maximum(jnp.max(scores, -1, keepdims=True), self_score)
    raw = jnp.exp(scores - peak)
    self_raw = jnp.exp(self_score - peak)
    denom = jnp.sum(raw, -1, keepdims=True) + self_raw
    weights = (raw / denom).astype(bf16)
    self_weight = (self_raw / denom).astype(bf16).astype(f32)
    attended = lax.dot_general(
        weights, values_ref[...], (((2,), (1,)), ((0,), (0,))), preferred_element_type=f32
    )
    attended = (attended + self_weight * new_value[:, None, :]) * own_head[None]
    attended = jnp.sum(attended, 1).astype(bf16)
    quarter = count // 4
    sent = []
    for part in range(4):
        first = part * quarter
        columns = out_w_ref[:, first * width : (first + quarter) * width]
        projected = jnp.dot(attended, columns, preferred_element_type=f32)
        for k in range(quarter):
            held_ref[first + k] = projected[:, k * width : (k + 1) * width]
        source, target = (ref.at[pl.ds(first, quarter)] for ref in (held_ref, parts_ref))
        sent.append(pltpu.make_async_copy(source, target, arrived.at[3 + part]))
        sent[-1].start()
    for copy in sent:
        copy.wait()


def partial_logits(z, normed_ref, pieces, piece_refs):
    count = normed_ref.shape[1]
    upwards = 2 * lax.rem(z, 2) - 1
    total = None
    for offsets, piece_ref in zip(pieces, piece_refs):
        at = [lax.rem(z + k * upwards + count, count) for k in offsets]
        rows = [side_by_side([normed_ref[branch, k] for k in at]) for branch in range(2)]
        rows = jnp.concatenate(rows, 0)
        part = jnp.dot(rows, piece_ref[...], preferred_element_type=f32)
        total = part if total is None else total + part
    return total


def norm_kernel(place_ref, rows_ref, gain_ref, *refs):
    piece_refs, (normed_ref, part_ref) = refs[:-2], refs[-2:]
    count = gain_ref.shape[0]
    for branch in range(2):
        rows = rows_ref[branch * count : (branch + 1) * count].astype(f32)
        normed_ref[branch] = normalized(rows, gain_ref[...])
    part_ref[...] = partial_logits(place_ref[0], normed_ref, PIECES[:-1], piece_refs)


def logits_kernel(
    place_ref, normed_ref, part_ref, guidance_ref, noise_ref, piece_ref, perturbed_ref, mass_ref
):
    count = normed_ref.shape[1]
    streams = noise_ref.shape[0]
    total = part_ref[...] + partial_logits(place_ref[0], normed_ref, PIECES[-1:], [piece_ref])
    conditioned, unconditioned = total[:streams], total[streams:]
    guided = unconditioned + guidance_ref[...] * (conditioned - unconditioned)
    perturbed = guided + noise_ref[...]
    perturbed_ref[...] = perturbed
    width = perturbed.shape[1] // 2
    lane = lax.broadcasted_iota(jnp.int32, (width, width), 1)
    columns = jnp.zeros((width, width), f32)
    for book in range(2):
        codes = perturbed[:, book * width : (book + 1) * width]
        peak = jnp.max(codes, -1, keepdims=True)
        mass = jnp.log(jnp.sum(jnp.exp(codes - peak), -1, keepdims=True)) + peak
        mass = jnp.concatenate([mass, jnp.zeros((width - streams, 1), f32)], 0)
        columns = jnp.where(lane == book, mass, columns)
    mass = columns.T[:8]
    for k in range(count):
        mass_ref[k] = mass


def final_kernel(mass_ref, perturbed_ref, out_ref):
    streams = perturbed_ref.shape[0]
    masses = mass_ref[...]
    peak = jnp.max(masses, 0)
    total = jnp.log(jnp.sum(jnp.exp(masses - peak[None]), 0)) + peak
    width = total.shape[1]
    total = jnp.concatenate([total, jnp.zeros((width - 8, width), f32)], 0).T
    for book in range(2):
        codes = perturbed_ref[:, book * width : (book + 1) * width]
        out_ref[:, book, :] = codes - total[:streams, book : book + 1]


def vmem(count):
    return [pl.BlockSpec(memory_space=pltpu.VMEM)] * count


def body(
    hidden_in,
    attn_gain,
    w_qkv,
    w_out,
    cache_keys,
    cache_values,
    cache_len,
    text_len,
    final_gain,
    lm_head,
    guidance,
    uniforms,
):
    branch_index = lax.axis_index("cfg")
    z = lax.axis_index("dp")
    count = lax.axis_size("tp")
    streams, width = hidden_in.shape[1:]
    half_books = CB // 2
    block, copies = started(hidden_in[0], lm_head, count)
    heads = first_heads(block)
    blocks = exchange(copies, "tp")
    positions = jnp.arange(CACHE, dtype=jnp.int32)
    usable = (positions[None, :] < cache_len[:, None]) & (
        (branch_index == 0) | (positions[None, :] >= text_len[:, None])
    )
    small = jnp.concatenate([usable.astype(f32), attn_gain.reshape(count, width)], 0)
    noise = -jnp.log(-jnp.log(uniforms)).reshape(streams, half_books * width)
    parts = pl.pallas_call(
        attend_kernel,
        out_shape=jax.ShapeDtypeStruct((count, streams, width), f32),
        in_specs=vmem(5) + [pl.BlockSpec(memory_space=pltpu.HBM)],
        out_specs=pl.BlockSpec(memory_space=pl.ANY),
        scratch_shapes=[
            pltpu.VMEM((3, D, width), bf16),
            pltpu.VMEM((count, streams, width), f32),
            pltpu.SemaphoreType.DMA((7,)),
        ],
        compiler_params=pltpu.CompilerParams(vmem_limit_bytes=51456 << 10),
        cost_estimate=pl.CostEstimate(flops=2 * 10**11, bytes_accessed=50 << 20, transcendentals=10**5),
    )(
        blocks,
        small,
        cache_keys[0],
        cache_values[0],
        w_out,
        jnp.moveaxis(w_qkv, 1, 0),
    )
    shares = exchange(parts, "tp")
    held, from_same, swap = second_heads(*heads)
    residual_part = (hidden_in[0].astype(f32) + shares.sum(0)).astype(bf16)
    copies = jnp.broadcast_to(residual_part, (2 * count, streams, width))
    rows = exchange(copies, ("cfg", "tp"))
    from_same, swap = lax.optimization_barrier((from_same, swap))
    heads = (held, from_same, swap, third_heads(from_same))
    place = z[None].astype(jnp.int32)
    smem = [pl.BlockSpec(memory_space=pltpu.SMEM)]
    normed, part = pl.pallas_call(
        norm_kernel,
        out_shape=(
            jax.ShapeDtypeStruct((2, count, streams, width), bf16),
            jax.ShapeDtypeStruct((2 * streams, half_books * width), f32),
        ),
        in_specs=smem + vmem(1 + len(heads)),
        out_specs=tuple(vmem(2)),
        compiler_params=pltpu.CompilerParams(vmem_limit_bytes=8 << 20),
        cost_estimate=pl.CostEstimate(flops=2 * 10**10, bytes_accessed=50 << 20, transcendentals=64),
    )(place, rows, final_gain.reshape(count, 1, width), *heads[:-1])
    perturbed, mass = pl.pallas_call(
        logits_kernel,
        out_shape=(
            jax.ShapeDtypeStruct((streams, half_books * width), f32),
            jax.ShapeDtypeStruct((count, 8, width), f32),
        ),
        in_specs=smem + vmem(5),
        out_specs=tuple(vmem(2)),
        compiler_params=pltpu.CompilerParams(vmem_limit_bytes=8 << 20),
        cost_estimate=pl.CostEstimate(flops=10**8, bytes_accessed=2 << 20, transcendentals=10**4),
    )(place, normed, part, guidance[:, None], noise, heads[-1])
    masses = exchange(mass, "tp")
    sample_logprobs = pl.pallas_call(
        final_kernel,
        out_shape=jax.ShapeDtypeStruct((streams, half_books, width), f32),
        in_specs=vmem(2),
        out_specs=pl.BlockSpec(memory_space=pltpu.VMEM),
        compiler_params=pltpu.CompilerParams(vmem_limit_bytes=8 << 20),
    )(masses, perturbed)
    return (sample_logprobs, residual_part[None])


def solution(mesh):
    placed = (
        P("cfg", "dp", "tp"),
        P(),
        P(None, None, "tp"),
        P("tp", None),
        P("cfg", "dp", None, "tp"),
        P("cfg", "dp", None, "tp"),
        P("dp"),
        P("dp"),
        P(),
        P(None, "dp", "tp"),
        P("dp"),
        P("dp", "cfg", "tp"),
    )
    return jax.shard_map(
        body,
        mesh=mesh,
        in_specs=placed,
        out_specs=(P("dp", "cfg", "tp"), P("cfg", "dp", "tp")),
        check_vma=False,
    )
```

```python
import jax
import jax.numpy as jnp
from jax import lax
from jax.experimental import pallas as pl
from jax.experimental.pallas import tpu as pltpu
from jax.sharding import PartitionSpec as P

D = 2048
HEAD_DIM = 64
CB = 4
CACHE = 128

epsilon = 1e-05
far_below = -1e30

f32, bf16 = jnp.float32, jnp.bfloat16


def exchange(blocks, axis):
    return lax.all_to_all(blocks, axis, split_axis=0, concat_axis=0, tiled=True)


def start_kernel(hidden_ref, head_ref, block_ref, copies_ref, sent):
    count = copies_ref.shape[0]
    width = head_ref.shape[2]
    books = head_ref.shape[0] // 2
    branch = lax.axis_index("cfg")
    heads = [
        pltpu.make_async_copy(
            head_ref.at[branch * books + book],
            block_ref.at[:, pl.ds(book * width, width)],
            sent.at[count + book],
        )
        for book in range(books)
    ]
    copies = [
        pltpu.make_async_copy(hidden_ref, copies_ref.at[k], sent.at[k]) for k in range(count)
    ]
    for copy in heads + copies:
        copy.start()
    for copy in heads + copies:
        copy.wait()


def started(hidden, lm_head, count):
    books, features, width = lm_head.shape
    return pl.pallas_call(
        start_kernel,
        out_shape=(
            jax.ShapeDtypeStruct((features, books // 2 * width), lm_head.dtype),
            jax.ShapeDtypeStruct((count, *hidden.shape), hidden.dtype),
        ),
        in_specs=vmem(1) + [pl.BlockSpec(memory_space=pl.ANY)],
        out_specs=(vmem(1)[0], pl.BlockSpec(memory_space=pl.ANY)),
        scratch_shapes=[pltpu.SemaphoreType.DMA((count + books // 2,))],
        compiler_params=pltpu.CompilerParams(vmem_limit_bytes=55150 << 10),
        cost_estimate=pl.CostEstimate(flops=2 * 10**11, bytes_accessed=1 << 20, transcendentals=0),
    )(hidden, lm_head)


PIECES = ((0, 1, 4, 5), (2, 3, 6, 7), (-1, -2, -5, -6), (-3, -4, -7, -8))


def moved(array, steps):
    count = lax.axis_size("dp")
    route = []
    for target in range(count):
        source = target + steps if target % 2 else target - steps
        route.append((source % count, target))
    return lax.ppermute(array, "dp", route)


def join_kernel(*refs):
    pieces, out_ref, arrived = refs[:-2], refs[-2], refs[-1]
    copies, at = [], 0
    for k, piece in enumerate(pieces):
        target = out_ref.at[pl.ds(at, piece.shape[0])]
        copies.append(pltpu.make_async_copy(piece, target, arrived.at[k]))
        at += piece.shape[0]
    for copy in copies:
        copy.start()
    for copy in copies:
        copy.wait()


def joined(*pieces):
    rows = sum(piece.shape[0] for piece in pieces)
    return pl.pallas_call(
        join_kernel,
        out_shape=jax.ShapeDtypeStruct((rows, *pieces[0].shape[1:]), pieces[0].dtype),
        in_specs=[pl.BlockSpec(memory_space=pl.ANY)] * len(pieces),
        out_specs=vmem(1)[0],
        scratch_shapes=[pltpu.SemaphoreType.DMA((len(pieces),))],
        compiler_params=pltpu.CompilerParams(vmem_limit_bytes=8192 << 10),
        cost_estimate=pl.CostEstimate(flops=2 * 10**10, bytes_accessed=1 << 20, transcendentals=0),
    )(*pieces)


def first_heads(block):
    near = joined(block, moved(block, 1))
    return near, moved(near, 4)


def second_heads(near, far):
    held = joined(near, far)
    from_same = moved(held, 2)
    return held, from_same, moved(held, -1)


def third_heads(from_same):
    return moved(from_same, -1)


def normalized(rows, gain):
    count = rows.shape[0] * rows.shape[2]
    average = jnp.sum(jnp.sum(rows, 0), -1, keepdims=True) / count
    apart = rows - average[None]
    spread = jnp.sum(jnp.sum(apart * apart, 0), -1, keepdims=True) / count
    return (apart * lax.rsqrt(spread + epsilon)[None] * gain).astype(bf16)


def side_by_side(blocks):
    return jnp.concatenate(blocks, axis=-1)


def attend_kernel(
    blocks_ref,
    small_ref,
    keys_ref,
    values_ref,
    out_w_ref,
    qkv_in,
    parts_ref,
    qkv_ref,
    held_ref,
    arrived,
):
    count, streams, width = blocks_ref.shape
    copies = [
        pltpu.make_async_copy(qkv_in.at[slot], qkv_ref.at[slot], arrived.at[slot])
        for slot in range(3)
    ]
    for copy in copies:
        copy.start()
    gain = small_ref[streams:][:, None, :]
    tokens = normalized(blocks_ref[...].astype(f32), gain)
    tokens = side_by_side([tokens[k] for k in range(count)])
    projections = []
    for slot in range(3):
        copies[slot].wait()
        slot_rows = jnp.dot(tokens, qkv_ref[slot], preferred_element_type=f32)
        projections.append(slot_rows.astype(bf16).astype(f32))
    query, new_key, new_value = projections
    head_of_lane = lax.broadcasted_iota(jnp.int32, (8, width), 1) // HEAD_DIM
    own_head = (head_of_lane == lax.broadcasted_iota(jnp.int32, (8, width), 0)).astype(f32)
    queries = query[:, None, :] * own_head[None]
    inv_root = 1.0 / HEAD_DIM**0.5
    scores = (
        lax.dot_general(
            queries.astype(bf16),
            keys_ref[...],
            (((2,), (2,)), ((0,), (0,))),
            preferred_element_type=f32,
        )
        * inv_root
    )
    scores = jnp.where(small_ref[:streams][:, None, :] > 0, scores, far_below)
    self_score = jnp.sum(queries * new_key[:, None, :], -1, keepdims=True) * inv_root
    peak = jnp.maximum(jnp.max(scores, -1, keepdims=True), self_score)
    raw = jnp.exp(scores - peak)
    self_raw = jnp.exp(self_score - peak)
    denom = jnp.sum(raw, -1, keepdims=True) + self_raw
    weights = (raw / denom).astype(bf16)
    self_weight = (self_raw / denom).astype(bf16).astype(f32)
    attended = lax.dot_general(
        weights, values_ref[...], (((2,), (1,)), ((0,), (0,))), preferred_element_type=f32
    )
    attended = (attended + self_weight * new_value[:, None, :]) * own_head[None]
    attended = jnp.sum(attended, 1).astype(bf16)
    quarter = count // 4
    sent = []
    for part in range(4):
        first = part * quarter
        columns = out_w_ref[:, first * width : (first + quarter) * width]
        projected = jnp.dot(attended, columns, preferred_element_type=f32)
        for k in range(quarter):
            held_ref[first + k] = projected[:, k * width : (k + 1) * width]
        source, target = (ref.at[pl.ds(first, quarter)] for ref in (held_ref, parts_ref))
        sent.append(pltpu.make_async_copy(source, target, arrived.at[3 + part]))
        sent[-1].start()
    for copy in sent:
        copy.wait()


def partial_logits(z, normed_ref, pieces, piece_refs):
    count = normed_ref.shape[1]
    upwards = 2 * lax.rem(z, 2) - 1
    total = None
    for offsets, piece_ref in zip(pieces, piece_refs):
        at = [lax.rem(z + k * upwards + count, count) for k in offsets]
        rows = [side_by_side([normed_ref[branch, k] for k in at]) for branch in range(2)]
        rows = jnp.concatenate(rows, 0)
        part = jnp.dot(rows, piece_ref[...], preferred_element_type=f32)
        total = part if total is None else total + part
    return total


def norm_kernel(place_ref, residual_ref, rows_ref, gain_ref, *refs):
    piece_refs, (normed_ref, part_ref, out_ref, sent) = refs[:-4], refs[-4:]
    copy = pltpu.make_async_copy(residual_ref, out_ref.at[0], sent)
    copy.start()
    count = gain_ref.shape[0]
    for branch in range(2):
        rows = rows_ref[branch * count : (branch + 1) * count].astype(f32)
        normed_ref[branch] = normalized(rows, gain_ref[...])
    part_ref[...] = partial_logits(place_ref[0], normed_ref, PIECES[:-1], piece_refs)
    copy.wait()


def logits_kernel(
    place_ref, normed_ref, part_ref, guidance_ref, noise_ref, piece_ref, perturbed_ref, mass_ref
):
    count = normed_ref.shape[1]
    streams = noise_ref.shape[0]
    total = part_ref[...] + partial_logits(place_ref[0], normed_ref, PIECES[-1:], [piece_ref])
    conditioned, unconditioned = total[:streams], total[streams:]
    guided = unconditioned + guidance_ref[...] * (conditioned - unconditioned)
    perturbed = guided + noise_ref[...]
    perturbed_ref[...] = perturbed
    width = perturbed.shape[1] // 2
    lane = lax.broadcasted_iota(jnp.int32, (width, width), 1)
    columns = jnp.zeros((width, width), f32)
    for book in range(2):
        codes = perturbed[:, book * width : (book + 1) * width]
        peak = jnp.max(codes, -1, keepdims=True)
        mass = jnp.log(jnp.sum(jnp.exp(codes - peak), -1, keepdims=True)) + peak
        mass = jnp.concatenate([mass, jnp.zeros((width - streams, 1), f32)], 0)
        columns = jnp.where(lane == book, mass, columns)
    mass = columns.T[:8]
    for k in range(count):
        mass_ref[k] = mass


def final_kernel(mass_ref, perturbed_ref, out_ref):
    streams = perturbed_ref.shape[0]
    masses = mass_ref[...]
    peak = jnp.max(masses, 0)
    total = jnp.log(jnp.sum(jnp.exp(masses - peak[None]), 0)) + peak
    width = total.shape[1]
    total = jnp.concatenate([total, jnp.zeros((width - 8, width), f32)], 0).T
    for book in range(2):
        codes = perturbed_ref[:, book * width : (book + 1) * width]
        out_ref[:, book, :] = codes - total[:streams, book : book + 1]


def vmem(count):
    return [pl.BlockSpec(memory_space=pltpu.VMEM)] * count


def body(
    hidden_in,
    attn_gain,
    w_qkv,
    w_out,
    cache_keys,
    cache_values,
    cache_len,
    text_len,
    final_gain,
    lm_head,
    guidance,
    uniforms,
):
    branch_index = lax.axis_index("cfg")
    z = lax.axis_index("dp")
    count = lax.axis_size("tp")
    streams, width = hidden_in.shape[1:]
    half_books = CB // 2
    block, copies = started(hidden_in[0], lm_head, count)
    heads = first_heads(block)
    blocks = exchange(copies, "tp")
    positions = jnp.arange(CACHE, dtype=jnp.int32)
    usable = (positions[None, :] < cache_len[:, None]) & (
        (branch_index == 0) | (positions[None, :] >= text_len[:, None])
    )
    small = jnp.concatenate([usable.astype(f32), attn_gain.reshape(count, width)], 0)
    noise = -jnp.log(-jnp.log(uniforms)).reshape(streams, half_books * width)
    parts = pl.pallas_call(
        attend_kernel,
        out_shape=jax.ShapeDtypeStruct((count, streams, width), f32),
        in_specs=vmem(5) + [pl.BlockSpec(memory_space=pltpu.HBM)],
        out_specs=pl.BlockSpec(memory_space=pl.ANY),
        scratch_shapes=[
            pltpu.VMEM((3, D, width), bf16),
            pltpu.VMEM((count, streams, width), f32),
            pltpu.SemaphoreType.DMA((7,)),
        ],
        compiler_params=pltpu.CompilerParams(vmem_limit_bytes=51456 << 10),
        cost_estimate=pl.CostEstimate(flops=2 * 10**11, bytes_accessed=50 << 20, transcendentals=10**5),
    )(
        blocks,
        small,
        cache_keys[0],
        cache_values[0],
        w_out,
        jnp.moveaxis(w_qkv, 1, 0),
    )
    shares = exchange(parts, "tp")
    held, from_same, swap = second_heads(*heads)
    residual_part = (hidden_in[0].astype(f32) + shares.sum(0)).astype(bf16)
    copies = jnp.broadcast_to(residual_part, (2 * count, streams, width))
    rows = exchange(copies, ("cfg", "tp"))
    from_same, swap = lax.optimization_barrier((from_same, swap))
    heads = (held, from_same, swap, third_heads(from_same))
    place = z[None].astype(jnp.int32)
    smem = [pl.BlockSpec(memory_space=pltpu.SMEM)]
    normed, part, residual_out = pl.pallas_call(
        norm_kernel,
        out_shape=(
            jax.ShapeDtypeStruct((2, count, streams, width), bf16),
            jax.ShapeDtypeStruct((2 * streams, half_books * width), f32),
            jax.ShapeDtypeStruct((1, streams, width), bf16),
        ),
        in_specs=smem + vmem(2 + len(heads)),
        out_specs=(*vmem(2), pl.BlockSpec(memory_space=pl.ANY)),
        scratch_shapes=[pltpu.SemaphoreType.DMA],
        compiler_params=pltpu.CompilerParams(vmem_limit_bytes=8 << 20),
        cost_estimate=pl.CostEstimate(flops=2 * 10**10, bytes_accessed=50 << 20, transcendentals=64),
    )(place, residual_part, rows, final_gain.reshape(count, 1, width), *heads[:-1])
    perturbed, mass = pl.pallas_call(
        logits_kernel,
        out_shape=(
            jax.ShapeDtypeStruct((streams, half_books * width), f32),
            jax.ShapeDtypeStruct((count, 8, width), f32),
        ),
        in_specs=smem + vmem(5),
        out_specs=tuple(vmem(2)),
        compiler_params=pltpu.CompilerParams(vmem_limit_bytes=8 << 20),
        cost_estimate=pl.CostEstimate(flops=10**8, bytes_accessed=2 << 20, transcendentals=10**4),
    )(place, normed, part, guidance[:, None], noise, heads[-1])
    masses = exchange(mass, "tp")
    sample_logprobs = pl.pallas_call(
        final_kernel,
        out_shape=jax.ShapeDtypeStruct((streams, half_books, width), f32),
        in_specs=vmem(2),
        out_specs=pl.BlockSpec(memory_space=pltpu.VMEM),
        compiler_params=pltpu.CompilerParams(vmem_limit_bytes=8 << 20),
    )(masses, perturbed)
    return (sample_logprobs, residual_out)


def solution(mesh):
    placed = (
        P("cfg", "dp", "tp"),
        P(),
        P(None, None, "tp"),
        P("tp", None),
        P("cfg", "dp", None, "tp"),
        P("cfg", "dp", None, "tp"),
        P("dp"),
        P("dp"),
        P(),
        P(None, "dp", "tp"),
        P("dp"),
        P("dp", "cfg", "tp"),
    )
    return jax.shard_map(
        body,
        mesh=mesh,
        in_specs=placed,
        out_specs=(P("dp", "cfg", "tp"), P("cfg", "dp", "tp")),
        check_vma=False,
    )
```

```python
import jax
import jax.numpy as jnp
from jax import lax
from jax.experimental import pallas as pl
from jax.experimental.pallas import tpu as pltpu
from jax.sharding import PartitionSpec as P

D = 2048
HEAD_DIM = 64
CB = 4
CACHE = 128

epsilon = 1e-05
far_below = -1e30

f32, bf16 = jnp.float32, jnp.bfloat16


def exchange(blocks, axis):
    return lax.all_to_all(blocks, axis, split_axis=0, concat_axis=0, tiled=True)


def start_kernel(hidden_ref, head_ref, block_ref, copies_ref, held_ref, sent):
    count = copies_ref.shape[0]
    width = head_ref.shape[2]
    books = head_ref.shape[0] // 2
    branch = lax.axis_index("cfg")
    heads = [
        pltpu.make_async_copy(
            head_ref.at[branch * books + book],
            block_ref.at[:, pl.ds(book * width, width)],
            sent.at[count + book],
        )
        for book in range(books)
    ]
    hidden = pltpu.make_async_copy(hidden_ref, held_ref, sent.at[count + books])
    hidden.start()
    for copy in heads:
        copy.start()
    hidden.wait()
    copies = [
        pltpu.make_async_copy(held_ref, copies_ref.at[k], sent.at[k]) for k in range(count)
    ]
    for copy in copies:
        copy.start()
    for copy in heads + copies:
        copy.wait()


def started(hidden, lm_head, count):
    books, features, width = lm_head.shape
    return pl.pallas_call(
        start_kernel,
        out_shape=(
            jax.ShapeDtypeStruct((features, books // 2 * width), lm_head.dtype),
            jax.ShapeDtypeStruct((count, *hidden.shape), hidden.dtype),
        ),
        in_specs=[pl.BlockSpec(memory_space=pltpu.HBM)] * 2,
        out_specs=(vmem(1)[0], pl.BlockSpec(memory_space=pl.ANY)),
        scratch_shapes=[
            pltpu.VMEM(hidden.shape, hidden.dtype),
            pltpu.SemaphoreType.DMA((count + books // 2 + 1,)),
        ],
        compiler_params=pltpu.CompilerParams(vmem_limit_bytes=8192 << 10),
        cost_estimate=pl.CostEstimate(flops=2 * 10**11, bytes_accessed=1 << 20, transcendentals=0),
    )(*(pltpu.with_memory_space_constraint(array, pltpu.HBM) for array in (hidden, lm_head)))


PIECES = ((0, 1, 4, 5), (2, 3, 6, 7), (-1, -2, -5, -6), (-3, -4, -7, -8))


def moved(array, steps):
    count = lax.axis_size("dp")
    route = []
    for target in range(count):
        source = target + steps if target % 2 else target - steps
        route.append((source % count, target))
    return lax.ppermute(array, "dp", route)


def join_kernel(*refs):
    pieces, out_ref, arrived = refs[:-2], refs[-2], refs[-1]
    copies, at = [], 0
    for k, piece in enumerate(pieces):
        target = out_ref.at[pl.ds(at, piece.shape[0])]
        copies.append(pltpu.make_async_copy(piece, target, arrived.at[k]))
        at += piece.shape[0]
    for copy in copies:
        copy.start()
    for copy in copies:
        copy.wait()


def joined(*pieces):
    rows = sum(piece.shape[0] for piece in pieces)
    return pl.pallas_call(
        join_kernel,
        out_shape=jax.ShapeDtypeStruct((rows, *pieces[0].shape[1:]), pieces[0].dtype),
        in_specs=[pl.BlockSpec(memory_space=pl.ANY)] * len(pieces),
        out_specs=vmem(1)[0],
        scratch_shapes=[pltpu.SemaphoreType.DMA((len(pieces),))],
        compiler_params=pltpu.CompilerParams(vmem_limit_bytes=8192 << 10),
        cost_estimate=pl.CostEstimate(flops=2 * 10**10, bytes_accessed=1 << 20, transcendentals=0),
    )(*pieces)


def first_heads(block):
    near = joined(block, moved(block, 1))
    return near, moved(near, 4)


def second_heads(near, far):
    held = joined(near, far)
    from_same = moved(held, 2)
    return held, from_same, moved(held, -1)


def third_heads(from_same):
    return moved(from_same, -1)


def normalized(rows, gain):
    count = rows.shape[0] * rows.shape[2]
    average = jnp.sum(jnp.sum(rows, 0), -1, keepdims=True) / count
    apart = rows - average[None]
    spread = jnp.sum(jnp.sum(apart * apart, 0), -1, keepdims=True) / count
    return (apart * lax.rsqrt(spread + epsilon)[None] * gain).astype(bf16)


def side_by_side(blocks):
    return jnp.concatenate(blocks, axis=-1)


def attend_kernel(
    blocks_ref,
    small_ref,
    qkv_ref,
    keys_ref,
    out_w_ref,
    values_in,
    parts_ref,
    values_ref,
    held_ref,
    arrived,
):
    count, streams, width = blocks_ref.shape
    values_copy = pltpu.make_async_copy(values_in, values_ref, arrived.at[4])
    values_copy.start()
    gain = small_ref[streams:][:, None, :]
    tokens = normalized(blocks_ref[...].astype(f32), gain)
    tokens = side_by_side([tokens[k] for k in range(count)])
    projections = []
    for slot in range(3):
        slot_rows = jnp.dot(tokens, qkv_ref[slot], preferred_element_type=f32)
        projections.append(slot_rows.astype(bf16).astype(f32))
    query, new_key, new_value = projections
    head_of_lane = lax.broadcasted_iota(jnp.int32, (8, width), 1) // HEAD_DIM
    own_head = (head_of_lane == lax.broadcasted_iota(jnp.int32, (8, width), 0)).astype(f32)
    queries = query[:, None, :] * own_head[None]
    inv_root = 1.0 / HEAD_DIM**0.5
    scores = (
        lax.dot_general(
            queries.astype(bf16),
            keys_ref[...],
            (((2,), (2,)), ((0,), (0,))),
            preferred_element_type=f32,
        )
        * inv_root
    )
    scores = jnp.where(small_ref[:streams][:, None, :] > 0, scores, far_below)
    self_score = jnp.sum(queries * new_key[:, None, :], -1, keepdims=True) * inv_root
    peak = jnp.maximum(jnp.max(scores, -1, keepdims=True), self_score)
    raw = jnp.exp(scores - peak)
    self_raw = jnp.exp(self_score - peak)
    denom = jnp.sum(raw, -1, keepdims=True) + self_raw
    weights = (raw / denom).astype(bf16)
    self_weight = (self_raw / denom).astype(bf16).astype(f32)
    values_copy.wait()
    attended = lax.dot_general(
        weights, values_ref[...], (((2,), (1,)), ((0,), (0,))), preferred_element_type=f32
    )
    attended = (attended + self_weight * new_value[:, None, :]) * own_head[None]
    attended = jnp.sum(attended, 1).astype(bf16)
    quarter = count // 4
    sent = []
    for part in range(4):
        first = part * quarter
        columns = out_w_ref[:, first * width : (first + quarter) * width]
        projected = jnp.dot(attended, columns, preferred_element_type=f32)
        for k in range(quarter):
            held_ref[first + k] = projected[:, k * width : (k + 1) * width]
        source, target = (ref.at[pl.ds(first, quarter)] for ref in (held_ref, parts_ref))
        sent.append(pltpu.make_async_copy(source, target, arrived.at[part]))
        sent[-1].start()
    for copy in sent:
        copy.wait()


def partial_logits(z, normed_ref, pieces, piece_refs):
    count = normed_ref.shape[1]
    upwards = 2 * lax.rem(z, 2) - 1
    total = None
    for offsets, piece_ref in zip(pieces, piece_refs):
        at = [lax.rem(z + k * upwards + count, count) for k in offsets]
        rows = [side_by_side([normed_ref[branch, k] for k in at]) for branch in range(2)]
        rows = jnp.concatenate(rows, 0)
        part = jnp.dot(rows, piece_ref[...], preferred_element_type=f32)
        total = part if total is None else total + part
    return total


def norm_kernel(place_ref, residual_ref, rows_ref, gain_ref, *refs):
    piece_refs, (normed_ref, part_ref, out_ref, sent) = refs[:-4], refs[-4:]
    copy = pltpu.make_async_copy(residual_ref, out_ref.at[0], sent)
    copy.start()
    count = gain_ref.shape[0]
    for branch in range(2):
        rows = rows_ref[branch * count : (branch + 1) * count].astype(f32)
        normed_ref[branch] = normalized(rows, gain_ref[...])
    part_ref[...] = partial_logits(place_ref[0], normed_ref, PIECES[:-1], piece_refs)
    copy.wait()


def logits_kernel(
    place_ref, normed_ref, part_ref, guidance_ref, noise_ref, piece_ref, perturbed_ref, mass_ref
):
    count = normed_ref.shape[1]
    streams = noise_ref.shape[0]
    total = part_ref[...] + partial_logits(place_ref[0], normed_ref, PIECES[-1:], [piece_ref])
    conditioned, unconditioned = total[:streams], total[streams:]
    guided = unconditioned + guidance_ref[...] * (conditioned - unconditioned)
    perturbed = guided + noise_ref[...]
    perturbed_ref[...] = perturbed
    width = perturbed.shape[1] // 2
    lane = lax.broadcasted_iota(jnp.int32, (width, width), 1)
    columns = jnp.zeros((width, width), f32)
    for book in range(2):
        codes = perturbed[:, book * width : (book + 1) * width]
        peak = jnp.max(codes, -1, keepdims=True)
        mass = jnp.log(jnp.sum(jnp.exp(codes - peak), -1, keepdims=True)) + peak
        mass = jnp.concatenate([mass, jnp.zeros((width - streams, 1), f32)], 0)
        columns = jnp.where(lane == book, mass, columns)
    mass = columns.T[:8]
    for k in range(count):
        mass_ref[k] = mass


def final_kernel(mass_ref, perturbed_ref, out_ref):
    streams = perturbed_ref.shape[0]
    masses = mass_ref[...]
    peak = jnp.max(masses, 0)
    total = jnp.log(jnp.sum(jnp.exp(masses - peak[None]), 0)) + peak
    width = total.shape[1]
    total = jnp.concatenate([total, jnp.zeros((width - 8, width), f32)], 0).T
    for book in range(2):
        codes = perturbed_ref[:, book * width : (book + 1) * width]
        out_ref[:, book, :] = codes - total[:streams, book : book + 1]


def vmem(count):
    return [pl.BlockSpec(memory_space=pltpu.VMEM)] * count


def body(
    hidden_in,
    attn_gain,
    w_qkv,
    w_out,
    cache_keys,
    cache_values,
    cache_len,
    text_len,
    final_gain,
    lm_head,
    guidance,
    uniforms,
):
    branch_index = lax.axis_index("cfg")
    z = lax.axis_index("dp")
    count = lax.axis_size("tp")
    streams, width = hidden_in.shape[1:]
    half_books = CB // 2
    block, copies = started(hidden_in[0], lm_head, count)
    heads = first_heads(block)
    blocks = exchange(copies, "tp")
    positions = jnp.arange(CACHE, dtype=jnp.int32)
    usable = (positions[None, :] < cache_len[:, None]) & (
        (branch_index == 0) | (positions[None, :] >= text_len[:, None])
    )
    small = jnp.concatenate([usable.astype(f32), attn_gain.reshape(count, width)], 0)
    noise = -jnp.log(-jnp.log(uniforms)).reshape(streams, half_books * width)
    parts = pl.pallas_call(
        attend_kernel,
        out_shape=jax.ShapeDtypeStruct((count, streams, width), f32),
        in_specs=vmem(5) + [pl.BlockSpec(memory_space=pltpu.HBM)],
        out_specs=pl.BlockSpec(memory_space=pl.ANY),
        scratch_shapes=[
            pltpu.VMEM(cache_values.shape[1:], bf16),
            pltpu.VMEM((count, streams, width), f32),
            pltpu.SemaphoreType.DMA((5,)),
        ],
        compiler_params=pltpu.CompilerParams(vmem_limit_bytes=16384 << 10),
        cost_estimate=pl.CostEstimate(flops=2 * 10**11, bytes_accessed=50 << 20, transcendentals=10**5),
    )(
        blocks,
        small,
        jnp.moveaxis(w_qkv, 1, 0),
        cache_keys[0],
        w_out,
        pltpu.with_memory_space_constraint(cache_values[0], pltpu.HBM),
    )
    shares = exchange(parts, "tp")
    held, from_same, swap = second_heads(*heads)
    residual_part = (hidden_in[0].astype(f32) + shares.sum(0)).astype(bf16)
    copies = jnp.broadcast_to(residual_part, (2 * count, streams, width))
    rows = exchange(copies, ("cfg", "tp"))
    from_same, swap = lax.optimization_barrier((from_same, swap))
    heads = (held, from_same, swap, third_heads(from_same))
    place = z[None].astype(jnp.int32)
    smem = [pl.BlockSpec(memory_space=pltpu.SMEM)]
    normed, part, residual_out = pl.pallas_call(
        norm_kernel,
        out_shape=(
            jax.ShapeDtypeStruct((2, count, streams, width), bf16),
            jax.ShapeDtypeStruct((2 * streams, half_books * width), f32),
            jax.ShapeDtypeStruct((1, streams, width), bf16),
        ),
        in_specs=smem + vmem(2 + len(heads)),
        out_specs=(*vmem(2), pl.BlockSpec(memory_space=pl.ANY)),
        scratch_shapes=[pltpu.SemaphoreType.DMA],
        compiler_params=pltpu.CompilerParams(vmem_limit_bytes=8 << 20),
        cost_estimate=pl.CostEstimate(flops=2 * 10**10, bytes_accessed=50 << 20, transcendentals=64),
    )(place, residual_part, rows, final_gain.reshape(count, 1, width), *heads[:-1])
    perturbed, mass = pl.pallas_call(
        logits_kernel,
        out_shape=(
            jax.ShapeDtypeStruct((streams, half_books * width), f32),
            jax.ShapeDtypeStruct((count, 8, width), f32),
        ),
        in_specs=smem + vmem(5),
        out_specs=tuple(vmem(2)),
        compiler_params=pltpu.CompilerParams(vmem_limit_bytes=8 << 20),
        cost_estimate=pl.CostEstimate(flops=10**8, bytes_accessed=2 << 20, transcendentals=10**4),
    )(place, normed, part, guidance[:, None], noise, heads[-1])
    masses = exchange(mass, "tp")
    sample_logprobs = pl.pallas_call(
        final_kernel,
        out_shape=jax.ShapeDtypeStruct((streams, half_books, width), f32),
        in_specs=vmem(2),
        out_specs=pl.BlockSpec(memory_space=pltpu.VMEM),
        compiler_params=pltpu.CompilerParams(vmem_limit_bytes=8 << 20),
    )(masses, perturbed)
    return (sample_logprobs, residual_out)


def solution(mesh):
    placed = (
        P("cfg", "dp", "tp"),
        P(),
        P(None, None, "tp"),
        P("tp", None),
        P("cfg", "dp", None, "tp"),
        P("cfg", "dp", None, "tp"),
        P("dp"),
        P("dp"),
        P(),
        P(None, "dp", "tp"),
        P("dp"),
        P("dp", "cfg", "tp"),
    )
    return jax.shard_map(
        body,
        mesh=mesh,
        in_specs=placed,
        out_specs=(P("dp", "cfg", "tp"), P("cfg", "dp", "tp")),
        check_vma=False,
    )
```

```python
import jax
import jax.numpy as jnp
from jax import lax
from jax.experimental import pallas as pl
from jax.experimental.pallas import tpu as pltpu
from jax.sharding import PartitionSpec as P

D = 2048
HEAD_DIM = 64
CB = 4
CACHE = 128

epsilon = 1e-05
far_below = -1e30

f32, bf16 = jnp.float32, jnp.bfloat16


def exchange(blocks, axis):
    return lax.all_to_all(blocks, axis, split_axis=0, concat_axis=0, tiled=True)


def start_kernel(hidden_ref, head_ref, block_ref, copies_ref, held_ref, sent):
    count = copies_ref.shape[0]
    width = head_ref.shape[2]
    books = head_ref.shape[0] // 2
    branch = lax.axis_index("cfg")
    heads = [
        pltpu.make_async_copy(
            head_ref.at[branch * books + book],
            block_ref.at[:, pl.ds(book * width, width)],
            sent.at[count + book],
        )
        for book in range(books)
    ]
    hidden = pltpu.make_async_copy(hidden_ref, held_ref, sent.at[count + books])
    hidden.start()
    for copy in heads:
        copy.start()
    hidden.wait()
    copies = [
        pltpu.make_async_copy(held_ref, copies_ref.at[k], sent.at[k]) for k in range(count)
    ]
    for copy in copies:
        copy.start()
    for copy in heads + copies:
        copy.wait()


def started(hidden, lm_head, count):
    books, features, width = lm_head.shape
    return pl.pallas_call(
        start_kernel,
        out_shape=(
            jax.ShapeDtypeStruct((features, books // 2 * width), lm_head.dtype),
            jax.ShapeDtypeStruct((count, *hidden.shape), hidden.dtype),
        ),
        in_specs=[pl.BlockSpec(memory_space=pltpu.HBM)] * 2,
        out_specs=(vmem(1)[0], pl.BlockSpec(memory_space=pl.ANY)),
        scratch_shapes=[
            pltpu.VMEM(hidden.shape, hidden.dtype),
            pltpu.SemaphoreType.DMA((count + books // 2 + 1,)),
        ],
        compiler_params=pltpu.CompilerParams(vmem_limit_bytes=8192 << 10),
        cost_estimate=pl.CostEstimate(flops=2 * 10**11, bytes_accessed=1 << 20, transcendentals=0),
    )(*(pltpu.with_memory_space_constraint(array, pltpu.HBM) for array in (hidden, lm_head)))


PIECES = ((0, 1, 4, 5), (2, 3, 6, 7), (-1, -2, -5, -6), (-3, -4, -7, -8))


def moved(array, steps):
    count = lax.axis_size("dp")
    route = []
    for target in range(count):
        source = target + steps if target % 2 else target - steps
        route.append((source % count, target))
    return lax.ppermute(array, "dp", route)


def join_kernel(*refs):
    pieces, out_ref, arrived = refs[:-2], refs[-2], refs[-1]
    copies, at = [], 0
    for k, piece in enumerate(pieces):
        target = out_ref.at[pl.ds(at, piece.shape[0])]
        copies.append(pltpu.make_async_copy(piece, target, arrived.at[k]))
        at += piece.shape[0]
    for copy in copies:
        copy.start()
    for copy in copies:
        copy.wait()


def joined(*pieces):
    rows = sum(piece.shape[0] for piece in pieces)
    return pl.pallas_call(
        join_kernel,
        out_shape=jax.ShapeDtypeStruct((rows, *pieces[0].shape[1:]), pieces[0].dtype),
        in_specs=[pl.BlockSpec(memory_space=pl.ANY)] * len(pieces),
        out_specs=vmem(1)[0],
        scratch_shapes=[pltpu.SemaphoreType.DMA((len(pieces),))],
        compiler_params=pltpu.CompilerParams(vmem_limit_bytes=8192 << 10),
        cost_estimate=pl.CostEstimate(flops=2 * 10**10, bytes_accessed=1 << 20, transcendentals=0),
    )(*pieces)


def first_heads(block):
    near = joined(block, moved(block, 1))
    return near, moved(near, 4)


def second_heads(near, far):
    held = joined(near, far)
    from_same = moved(held, 2)
    return held, from_same, moved(held, -1)


def third_heads(from_same):
    return moved(from_same, -1)


def normalized(rows, gain):
    count = rows.shape[0] * rows.shape[2]
    average = jnp.sum(jnp.sum(rows, 0), -1, keepdims=True) / count
    apart = rows - average[None]
    spread = jnp.sum(jnp.sum(apart * apart, 0), -1, keepdims=True) / count
    return (apart * lax.rsqrt(spread + epsilon)[None] * gain).astype(bf16)


def side_by_side(blocks):
    return jnp.concatenate(blocks, axis=-1)


def attend_kernel(
    blocks_ref,
    small_ref,
    qkv_ref,
    keys_ref,
    out_w_ref,
    values_in,
    parts_ref,
    values_ref,
    held_ref,
    arrived,
):
    count, streams, width = blocks_ref.shape
    values_copy = pltpu.make_async_copy(values_in, values_ref, arrived.at[4])
    values_copy.start()
    gain = small_ref[streams:][:, None, :]
    tokens = normalized(blocks_ref[...].astype(f32), gain)
    tokens = side_by_side([tokens[k] for k in range(count)])
    weights = side_by_side([qkv_ref[slot] for slot in range(3)])
    projected = jnp.dot(tokens, weights, preferred_element_type=f32).astype(bf16).astype(f32)
    query, new_key, new_value = (
        projected[:, slot * width : (slot + 1) * width] for slot in range(3)
    )
    head_of_lane = lax.broadcasted_iota(jnp.int32, (8, width), 1) // HEAD_DIM
    own_head = (head_of_lane == lax.broadcasted_iota(jnp.int32, (8, width), 0)).astype(f32)
    queries = query[:, None, :] * own_head[None]
    inv_root = 1.0 / HEAD_DIM**0.5
    scores = (
        lax.dot_general(
            queries.astype(bf16),
            keys_ref[...],
            (((2,), (2,)), ((0,), (0,))),
            preferred_element_type=f32,
        )
        * inv_root
    )
    scores = jnp.where(small_ref[:streams][:, None, :] > 0, scores, far_below)
    self_score = jnp.sum(queries * new_key[:, None, :], -1, keepdims=True) * inv_root
    peak = jnp.maximum(jnp.max(scores, -1, keepdims=True), self_score)
    raw = jnp.exp(scores - peak)
    self_raw = jnp.exp(self_score - peak)
    denom = jnp.sum(raw, -1, keepdims=True) + self_raw
    weights = (raw / denom).astype(bf16)
    self_weight = (self_raw / denom).astype(bf16).astype(f32)
    values_copy.wait()
    attended = lax.dot_general(
        weights, values_ref[...], (((2,), (1,)), ((0,), (0,))), preferred_element_type=f32
    )
    attended = (attended + self_weight * new_value[:, None, :]) * own_head[None]
    attended = jnp.sum(attended, 1).astype(bf16)
    quarter = count // 4
    sent = []
    for part in range(4):
        first = part * quarter
        columns = out_w_ref[:, first * width : (first + quarter) * width]
        projected = jnp.dot(attended, columns, preferred_element_type=f32)
        for k in range(quarter):
            held_ref[first + k] = projected[:, k * width : (k + 1) * width]
        source, target = (ref.at[pl.ds(first, quarter)] for ref in (held_ref, parts_ref))
        sent.append(pltpu.make_async_copy(source, target, arrived.at[part]))
        sent[-1].start()
    for copy in sent:
        copy.wait()


def partial_logits(z, normed_ref, pieces, piece_refs):
    count = normed_ref.shape[1]
    upwards = 2 * lax.rem(z, 2) - 1
    total = None
    for offsets, piece_ref in zip(pieces, piece_refs):
        at = [lax.rem(z + k * upwards + count, count) for k in offsets]
        rows = [side_by_side([normed_ref[branch, k] for k in at]) for branch in range(2)]
        rows = jnp.concatenate(rows, 0)
        part = jnp.dot(rows, piece_ref[...], preferred_element_type=f32)
        total = part if total is None else total + part
    return total


def norm_kernel(place_ref, residual_ref, rows_ref, gain_ref, *refs):
    piece_refs, (normed_ref, part_ref, out_ref, sent) = refs[:-4], refs[-4:]
    copy = pltpu.make_async_copy(residual_ref, out_ref.at[0], sent)
    copy.start()
    count = gain_ref.shape[0]
    for branch in range(2):
        rows = rows_ref[branch * count : (branch + 1) * count].astype(f32)
        normed_ref[branch] = normalized(rows, gain_ref[...])
    part_ref[...] = partial_logits(place_ref[0], normed_ref, PIECES[:-1], piece_refs)
    copy.wait()


def logits_kernel(
    place_ref, normed_ref, part_ref, guidance_ref, noise_ref, piece_ref, perturbed_ref, mass_ref
):
    count = normed_ref.shape[1]
    streams = noise_ref.shape[0]
    total = part_ref[...] + partial_logits(place_ref[0], normed_ref, PIECES[-1:], [piece_ref])
    conditioned, unconditioned = total[:streams], total[streams:]
    guided = unconditioned + guidance_ref[...] * (conditioned - unconditioned)
    perturbed = guided + noise_ref[...]
    perturbed_ref[...] = perturbed
    width = perturbed.shape[1] // 2
    lane = lax.broadcasted_iota(jnp.int32, (width, width), 1)
    columns = jnp.zeros((width, width), f32)
    for book in range(2):
        codes = perturbed[:, book * width : (book + 1) * width]
        peak = jnp.max(codes, -1, keepdims=True)
        mass = jnp.log(jnp.sum(jnp.exp(codes - peak), -1, keepdims=True)) + peak
        mass = jnp.concatenate([mass, jnp.zeros((width - streams, 1), f32)], 0)
        columns = jnp.where(lane == book, mass, columns)
    mass = columns.T[:8]
    for k in range(count):
        mass_ref[k] = mass


def final_kernel(mass_ref, perturbed_ref, out_ref):
    streams = perturbed_ref.shape[0]
    masses = mass_ref[...]
    peak = jnp.max(masses, 0)
    total = jnp.log(jnp.sum(jnp.exp(masses - peak[None]), 0)) + peak
    width = total.shape[1]
    total = jnp.concatenate([total, jnp.zeros((width - 8, width), f32)], 0).T
    for book in range(2):
        codes = perturbed_ref[:, book * width : (book + 1) * width]
        out_ref[:, book, :] = codes - total[:streams, book : book + 1]


def vmem(count):
    return [pl.BlockSpec(memory_space=pltpu.VMEM)] * count


def body(
    hidden_in,
    attn_gain,
    w_qkv,
    w_out,
    cache_keys,
    cache_values,
    cache_len,
    text_len,
    final_gain,
    lm_head,
    guidance,
    uniforms,
):
    branch_index = lax.axis_index("cfg")
    z = lax.axis_index("dp")
    count = lax.axis_size("tp")
    streams, width = hidden_in.shape[1:]
    half_books = CB // 2
    block, copies = started(hidden_in[0], lm_head, count)
    heads = first_heads(block)
    blocks = exchange(copies, "tp")
    positions = jnp.arange(CACHE, dtype=jnp.int32)
    usable = (positions[None, :] < cache_len[:, None]) & (
        (branch_index == 0) | (positions[None, :] >= text_len[:, None])
    )
    small = jnp.concatenate([usable.astype(f32), attn_gain.reshape(count, width)], 0)
    noise = -jnp.log(-jnp.log(uniforms)).reshape(streams, half_books * width)
    parts = pl.pallas_call(
        attend_kernel,
        out_shape=jax.ShapeDtypeStruct((count, streams, width), f32),
        in_specs=vmem(5) + [pl.BlockSpec(memory_space=pltpu.HBM)],
        out_specs=pl.BlockSpec(memory_space=pl.ANY),
        scratch_shapes=[
            pltpu.VMEM(cache_values.shape[1:], bf16),
            pltpu.VMEM((count, streams, width), f32),
            pltpu.SemaphoreType.DMA((5,)),
        ],
        compiler_params=pltpu.CompilerParams(vmem_limit_bytes=16384 << 10),
        cost_estimate=pl.CostEstimate(flops=2 * 10**11, bytes_accessed=50 << 20, transcendentals=10**5),
    )(
        blocks,
        small,
        jnp.moveaxis(w_qkv, 1, 0),
        cache_keys[0],
        w_out,
        pltpu.with_memory_space_constraint(cache_values[0], pltpu.HBM),
    )
    shares = exchange(parts, "tp")
    held, from_same, swap = second_heads(*heads)
    residual_part = (hidden_in[0].astype(f32) + shares.sum(0)).astype(bf16)
    copies = jnp.broadcast_to(residual_part, (2 * count, streams, width))
    rows = exchange(copies, ("cfg", "tp"))
    from_same, swap = lax.optimization_barrier((from_same, swap))
    heads = (held, from_same, swap, third_heads(from_same))
    place = z[None].astype(jnp.int32)
    smem = [pl.BlockSpec(memory_space=pltpu.SMEM)]
    normed, part, residual_out = pl.pallas_call(
        norm_kernel,
        out_shape=(
            jax.ShapeDtypeStruct((2, count, streams, width), bf16),
            jax.ShapeDtypeStruct((2 * streams, half_books * width), f32),
            jax.ShapeDtypeStruct((1, streams, width), bf16),
        ),
        in_specs=smem + vmem(2 + len(heads)),
        out_specs=(*vmem(2), pl.BlockSpec(memory_space=pl.ANY)),
        scratch_shapes=[pltpu.SemaphoreType.DMA],
        compiler_params=pltpu.CompilerParams(vmem_limit_bytes=8 << 20),
        cost_estimate=pl.CostEstimate(flops=2 * 10**10, bytes_accessed=50 << 20, transcendentals=64),
    )(place, residual_part, rows, final_gain.reshape(count, 1, width), *heads[:-1])
    perturbed, mass = pl.pallas_call(
        logits_kernel,
        out_shape=(
            jax.ShapeDtypeStruct((streams, half_books * width), f32),
            jax.ShapeDtypeStruct((count, 8, width), f32),
        ),
        in_specs=smem + vmem(5),
        out_specs=tuple(vmem(2)),
        compiler_params=pltpu.CompilerParams(vmem_limit_bytes=8 << 20),
        cost_estimate=pl.CostEstimate(flops=10**8, bytes_accessed=2 << 20, transcendentals=10**4),
    )(place, normed, part, guidance[:, None], noise, heads[-1])
    masses = exchange(mass, "tp")
    sample_logprobs = pl.pallas_call(
        final_kernel,
        out_shape=jax.ShapeDtypeStruct((streams, half_books, width), f32),
        in_specs=vmem(2),
        out_specs=pl.BlockSpec(memory_space=pltpu.VMEM),
        compiler_params=pltpu.CompilerParams(vmem_limit_bytes=8 << 20),
    )(masses, perturbed)
    return (sample_logprobs, residual_out)


def solution(mesh):
    placed = (
        P("cfg", "dp", "tp"),
        P(),
        P(None, None, "tp"),
        P("tp", None),
        P("cfg", "dp", None, "tp"),
        P("cfg", "dp", None, "tp"),
        P("dp"),
        P("dp"),
        P(),
        P(None, "dp", "tp"),
        P("dp"),
        P("dp", "cfg", "tp"),
    )
    return jax.shard_map(
        body,
        mesh=mesh,
        in_specs=placed,
        out_specs=(P("dp", "cfg", "tp"), P("cfg", "dp", "tp")),
        check_vma=False,
    )
```

```python
import jax
import jax.numpy as jnp
from jax import lax
from jax.experimental import pallas as pl
from jax.experimental.pallas import tpu as pltpu
from jax.sharding import PartitionSpec as P

D = 2048
HEAD_DIM = 64
CB = 4
CACHE = 128

epsilon = 1e-05
far_below = -1e30

f32, bf16 = jnp.float32, jnp.bfloat16


def exchange(blocks, axis):
    return lax.all_to_all(blocks, axis, split_axis=0, concat_axis=0, tiled=True)


def start_kernel(hidden_ref, head_ref, block_ref, copies_ref, held_ref, sent):
    count = copies_ref.shape[0]
    width = head_ref.shape[2]
    books = head_ref.shape[0] // 2
    branch = lax.axis_index("cfg")
    heads = [
        pltpu.make_async_copy(
            head_ref.at[branch * books + book],
            block_ref.at[:, pl.ds(book * width, width)],
            sent.at[count + book],
        )
        for book in range(books)
    ]
    hidden = pltpu.make_async_copy(hidden_ref, held_ref, sent.at[count + books])
    hidden.start()
    for copy in heads:
        copy.start()
    hidden.wait()
    copies = [
        pltpu.make_async_copy(held_ref, copies_ref.at[k], sent.at[k]) for k in range(count)
    ]
    for copy in copies:
        copy.start()
    for copy in heads + copies:
        copy.wait()


def started(hidden, lm_head, count):
    books, features, width = lm_head.shape
    return pl.pallas_call(
        start_kernel,
        out_shape=(
            jax.ShapeDtypeStruct((features, books // 2 * width), lm_head.dtype),
            jax.ShapeDtypeStruct((count, *hidden.shape), hidden.dtype),
        ),
        in_specs=[pl.BlockSpec(memory_space=pltpu.HBM)] * 2,
        out_specs=(vmem(1)[0], pl.BlockSpec(memory_space=pl.ANY)),
        scratch_shapes=[
            pltpu.VMEM(hidden.shape, hidden.dtype),
            pltpu.SemaphoreType.DMA((count + books // 2 + 1,)),
        ],
        compiler_params=pltpu.CompilerParams(vmem_limit_bytes=8192 << 10),
        cost_estimate=pl.CostEstimate(flops=2 * 10**11, bytes_accessed=1 << 20, transcendentals=0),
    )(*(pltpu.with_memory_space_constraint(array, pltpu.HBM) for array in (hidden, lm_head)))


PIECES = ((0, 1, 4, 5), (2, 3, 6, 7), (-1, -2, -5, -6), (-3, -4, -7, -8))


def moved(array, steps):
    count = lax.axis_size("dp")
    route = []
    for target in range(count):
        source = target + steps if target % 2 else target - steps
        route.append((source % count, target))
    return lax.ppermute(array, "dp", route)


def join_kernel(*refs):
    pieces, out_ref, arrived = refs[:-2], refs[-2], refs[-1]
    copies, at = [], 0
    for k, piece in enumerate(pieces):
        target = out_ref.at[pl.ds(at, piece.shape[0])]
        copies.append(pltpu.make_async_copy(piece, target, arrived.at[k]))
        at += piece.shape[0]
    for copy in copies:
        copy.start()
    for copy in copies:
        copy.wait()


def joined(*pieces):
    rows = sum(piece.shape[0] for piece in pieces)
    return pl.pallas_call(
        join_kernel,
        out_shape=jax.ShapeDtypeStruct((rows, *pieces[0].shape[1:]), pieces[0].dtype),
        in_specs=[pl.BlockSpec(memory_space=pl.ANY)] * len(pieces),
        out_specs=vmem(1)[0],
        scratch_shapes=[pltpu.SemaphoreType.DMA((len(pieces),))],
        compiler_params=pltpu.CompilerParams(vmem_limit_bytes=8192 << 10),
        cost_estimate=pl.CostEstimate(flops=2 * 10**10, bytes_accessed=1 << 20, transcendentals=0),
    )(*pieces)


def first_heads(block):
    near = joined(block, moved(block, 1))
    return near, moved(near, 4)


def second_heads(near, far):
    held = joined(near, far)
    from_same = moved(held, 2)
    return held, from_same, moved(held, -1)


def third_heads(from_same):
    return moved(from_same, -1)


def normalized(rows, gain):
    count = rows.shape[0] * rows.shape[2]
    average = jnp.sum(jnp.sum(rows, 0), -1, keepdims=True) / count
    apart = rows - average[None]
    spread = jnp.sum(jnp.sum(apart * apart, 0), -1, keepdims=True) / count
    return (apart * lax.rsqrt(spread + epsilon)[None] * gain).astype(bf16)


def side_by_side(blocks):
    return jnp.concatenate(blocks, axis=-1)


def attend_kernel(
    blocks_ref,
    small_ref,
    qkv_ref,
    keys_ref,
    out_w_ref,
    values_in,
    parts_ref,
    values_ref,
    held_ref,
    arrived,
):
    count, streams, width = blocks_ref.shape
    values_copy = pltpu.make_async_copy(values_in, values_ref, arrived.at[4])
    values_copy.start()
    gain = small_ref[streams:][:, None, :]
    tokens = normalized(blocks_ref[...].astype(f32), gain)
    tokens = side_by_side([tokens[k] for k in range(count)])
    projections = []
    for slot in range(3):
        slot_rows = jnp.dot(tokens, qkv_ref[slot], preferred_element_type=f32)
        projections.append(slot_rows.astype(bf16).astype(f32))
    query, new_key, new_value = projections
    head_of_lane = lax.broadcasted_iota(jnp.int32, (8, width), 1) // HEAD_DIM
    own_head = (head_of_lane == lax.broadcasted_iota(jnp.int32, (8, width), 0)).astype(f32)
    queries = query[:, None, :] * own_head[None]
    inv_root = 1.0 / HEAD_DIM**0.5
    scores = (
        lax.dot_general(
            queries.astype(bf16),
            keys_ref[...],
            (((2,), (2,)), ((0,), (0,))),
            preferred_element_type=f32,
        )
        * inv_root
    )
    scores = jnp.where(small_ref[:streams][:, None, :] > 0, scores, far_below)
    self_score = jnp.sum(queries * new_key[:, None, :], -1, keepdims=True) * inv_root
    peak = jnp.maximum(jnp.max(scores, -1, keepdims=True), self_score)
    raw = jnp.exp(scores - peak)
    self_raw = jnp.exp(self_score - peak)
    denom = jnp.sum(raw, -1, keepdims=True) + self_raw
    weights = (raw / denom).astype(bf16)
    self_weight = (self_raw / denom).astype(bf16).astype(f32)
    values_copy.wait()
    attended = lax.dot_general(
        weights, values_ref[...], (((2,), (1,)), ((0,), (0,))), preferred_element_type=f32
    )
    attended = (attended + self_weight * new_value[:, None, :]) * own_head[None]
    attended = jnp.sum(attended, 1).astype(bf16)
    half = count // 2
    sent = []
    for part in range(2):
        first = part * half
        columns = out_w_ref[:, first * width : (first + half) * width]
        projected = jnp.dot(attended, columns, preferred_element_type=f32)
        for k in range(half):
            held_ref[first + k] = projected[:, k * width : (k + 1) * width]
        source, target = (ref.at[pl.ds(first, half)] for ref in (held_ref, parts_ref))
        sent.append(pltpu.make_async_copy(source, target, arrived.at[part]))
        sent[-1].start()
    for copy in sent:
        copy.wait()


def partial_logits(z, normed_ref, pieces, piece_refs):
    count = normed_ref.shape[1]
    upwards = 2 * lax.rem(z, 2) - 1
    total = None
    for offsets, piece_ref in zip(pieces, piece_refs):
        at = [lax.rem(z + k * upwards + count, count) for k in offsets]
        rows = [side_by_side([normed_ref[branch, k] for k in at]) for branch in range(2)]
        rows = jnp.concatenate(rows, 0)
        part = jnp.dot(rows, piece_ref[...], preferred_element_type=f32)
        total = part if total is None else total + part
    return total


def norm_kernel(place_ref, residual_ref, rows_ref, gain_ref, *refs):
    piece_refs, (normed_ref, part_ref, out_ref, sent) = refs[:-4], refs[-4:]
    copy = pltpu.make_async_copy(residual_ref, out_ref.at[0], sent)
    copy.start()
    count = gain_ref.shape[0]
    for branch in range(2):
        rows = rows_ref[branch * count : (branch + 1) * count].astype(f32)
        normed_ref[branch] = normalized(rows, gain_ref[...])
    part_ref[...] = partial_logits(place_ref[0], normed_ref, PIECES[:-1], piece_refs)
    copy.wait()


def logits_kernel(
    place_ref, normed_ref, part_ref, guidance_ref, noise_ref, piece_ref, perturbed_ref, mass_ref
):
    count = normed_ref.shape[1]
    streams = noise_ref.shape[0]
    total = part_ref[...] + partial_logits(place_ref[0], normed_ref, PIECES[-1:], [piece_ref])
    conditioned, unconditioned = total[:streams], total[streams:]
    guided = unconditioned + guidance_ref[...] * (conditioned - unconditioned)
    perturbed = guided + noise_ref[...]
    perturbed_ref[...] = perturbed
    width = perturbed.shape[1] // 2
    lane = lax.broadcasted_iota(jnp.int32, (width, width), 1)
    columns = jnp.zeros((width, width), f32)
    for book in range(2):
        codes = perturbed[:, book * width : (book + 1) * width]
        peak = jnp.max(codes, -1, keepdims=True)
        mass = jnp.log(jnp.sum(jnp.exp(codes - peak), -1, keepdims=True)) + peak
        mass = jnp.concatenate([mass, jnp.zeros((width - streams, 1), f32)], 0)
        columns = jnp.where(lane == book, mass, columns)
    mass = columns.T[:8]
    for k in range(count):
        mass_ref[k] = mass


def final_kernel(mass_ref, perturbed_ref, out_ref):
    streams = perturbed_ref.shape[0]
    masses = mass_ref[...]
    peak = jnp.max(masses, 0)
    total = jnp.log(jnp.sum(jnp.exp(masses - peak[None]), 0)) + peak
    width = total.shape[1]
    total = jnp.concatenate([total, jnp.zeros((width - 8, width), f32)], 0).T
    for book in range(2):
        codes = perturbed_ref[:, book * width : (book + 1) * width]
        out_ref[:, book, :] = codes - total[:streams, book : book + 1]


def vmem(count):
    return [pl.BlockSpec(memory_space=pltpu.VMEM)] * count


def body(
    hidden_in,
    attn_gain,
    w_qkv,
    w_out,
    cache_keys,
    cache_values,
    cache_len,
    text_len,
    final_gain,
    lm_head,
    guidance,
    uniforms,
):
    branch_index = lax.axis_index("cfg")
    z = lax.axis_index("dp")
    count = lax.axis_size("tp")
    streams, width = hidden_in.shape[1:]
    half_books = CB // 2
    block, copies = started(hidden_in[0], lm_head, count)
    heads = first_heads(block)
    blocks = exchange(copies, "tp")
    positions = jnp.arange(CACHE, dtype=jnp.int32)
    usable = (positions[None, :] < cache_len[:, None]) & (
        (branch_index == 0) | (positions[None, :] >= text_len[:, None])
    )
    small = jnp.concatenate([usable.astype(f32), attn_gain.reshape(count, width)], 0)
    noise = -jnp.log(-jnp.log(uniforms)).reshape(streams, half_books * width)
    parts = pl.pallas_call(
        attend_kernel,
        out_shape=jax.ShapeDtypeStruct((count, streams, width), f32),
        in_specs=vmem(5) + [pl.BlockSpec(memory_space=pltpu.HBM)],
        out_specs=pl.BlockSpec(memory_space=pl.ANY),
        scratch_shapes=[
            pltpu.VMEM(cache_values.shape[1:], bf16),
            pltpu.VMEM((count, streams, width), f32),
            pltpu.SemaphoreType.DMA((5,)),
        ],
        compiler_params=pltpu.CompilerParams(vmem_limit_bytes=16384 << 10),
        cost_estimate=pl.CostEstimate(flops=2 * 10**11, bytes_accessed=50 << 20, transcendentals=10**5),
    )(
        blocks,
        small,
        jnp.moveaxis(w_qkv, 1, 0),
        cache_keys[0],
        w_out,
        pltpu.with_memory_space_constraint(cache_values[0], pltpu.HBM),
    )
    shares = exchange(parts, "tp")
    held, from_same, swap = second_heads(*heads)
    residual_part = (hidden_in[0].astype(f32) + shares.sum(0)).astype(bf16)
    copies = jnp.broadcast_to(residual_part, (2 * count, streams, width))
    rows = exchange(copies, ("cfg", "tp"))
    from_same, swap = lax.optimization_barrier((from_same, swap))
    heads = (held, from_same, swap, third_heads(from_same))
    place = z[None].astype(jnp.int32)
    smem = [pl.BlockSpec(memory_space=pltpu.SMEM)]
    normed, part, residual_out = pl.pallas_call(
        norm_kernel,
        out_shape=(
            jax.ShapeDtypeStruct((2, count, streams, width), bf16),
            jax.ShapeDtypeStruct((2 * streams, half_books * width), f32),
            jax.ShapeDtypeStruct((1, streams, width), bf16),
        ),
        in_specs=smem + vmem(2 + len(heads)),
        out_specs=(*vmem(2), pl.BlockSpec(memory_space=pl.ANY)),
        scratch_shapes=[pltpu.SemaphoreType.DMA],
        compiler_params=pltpu.CompilerParams(vmem_limit_bytes=8 << 20),
        cost_estimate=pl.CostEstimate(flops=2 * 10**10, bytes_accessed=50 << 20, transcendentals=64),
    )(place, residual_part, rows, final_gain.reshape(count, 1, width), *heads[:-1])
    perturbed, mass = pl.pallas_call(
        logits_kernel,
        out_shape=(
            jax.ShapeDtypeStruct((streams, half_books * width), f32),
            jax.ShapeDtypeStruct((count, 8, width), f32),
        ),
        in_specs=smem + vmem(5),
        out_specs=tuple(vmem(2)),
        compiler_params=pltpu.CompilerParams(vmem_limit_bytes=8 << 20),
        cost_estimate=pl.CostEstimate(flops=10**8, bytes_accessed=2 << 20, transcendentals=10**4),
    )(place, normed, part, guidance[:, None], noise, heads[-1])
    masses = exchange(mass, "tp")
    sample_logprobs = pl.pallas_call(
        final_kernel,
        out_shape=jax.ShapeDtypeStruct((streams, half_books, width), f32),
        in_specs=vmem(2),
        out_specs=pl.BlockSpec(memory_space=pltpu.VMEM),
        compiler_params=pltpu.CompilerParams(vmem_limit_bytes=8 << 20),
    )(masses, perturbed)
    return (sample_logprobs, residual_out)


def solution(mesh):
    placed = (
        P("cfg", "dp", "tp"),
        P(),
        P(None, None, "tp"),
        P("tp", None),
        P("cfg", "dp", None, "tp"),
        P("cfg", "dp", None, "tp"),
        P("dp"),
        P("dp"),
        P(),
        P(None, "dp", "tp"),
        P("dp"),
        P("dp", "cfg", "tp"),
    )
    return jax.shard_map(
        body,
        mesh=mesh,
        in_specs=placed,
        out_specs=(P("dp", "cfg", "tp"), P("cfg", "dp", "tp")),
        check_vma=False,
    )
```
